256 devices in a mesh: gx: 32 (over x, z_lo, core), ka: 8 (over y, z_hi).
Axes of the slice: x: 4, y: 4, z: 8 (z_hi: 2, z_lo: 4; z = z_hi * 4 + z_lo), core: 2. Of those that a mesh axis runs over, the one named last changes fastest.
Arguments:
- density: float32 [128, 64, 128, 128], P('gx', None, 'ka'), may hold values from -6 to 6
- potential_x: float32 [128, 128], P('gx'), may hold values from -6 to 6
- potential_y: float32 [64, 128], replicated, may hold values from -6 to 6
- speeds_x: float32 [128], P('ka'), may hold values from 0.2 to 1.5
- speeds_y: float32 [128], replicated, may hold values from 0.2 to 1.5
- upwind_x: int32 [128], P('ka'), may hold values from 0 to 1
- upwind_y: int32 [128], replicated, may hold values from 0 to 1
Outputs:
- advanced: float32 [128, 64, 128, 128], P('gx', None, 'ka')
The draws below stay inside these ranges and needn't reach their ends.
Inputs may be any that keep to these rules, and one draw needn't show every extreme that they name: `upwind_x`: 1 means drift toward higher positions, 0 toward lower. `upwind_y`: 1 means drift toward higher positions, 0 toward lower.
All inputs are finite; a program needn't handle non-finite values.
Results may differ from the reference program's by a relative error of at most 0.0003.
Values sent between devices are 32-bit elements; how exact they have to be, the bound alone decides.
No kernel may reach another device: no remote copies, remote signals or barrier semaphores. Data moves between devices by JAX's collectives and lax.ppermute only.
A program may use at most 64 MiB of HBM per device.

```python
import math
import jax
import jax.numpy as jnp
from jax import lax

Y = 64
KX = 128
KY = 128
X = 128


def place_ends(array, key, low, high):
    longest = array.shape.index(max(array.shape))
    spots = []
    for shift in (0, 1):
        where = [jax.random.randint(jax.random.fold_in(key, axis), (), 0, length) for axis, length in enumerate(array.shape)]
        where[longest] = (where[longest] + shift) % array.shape[longest]
        spots.append(tuple(where))
    return array.at[spots[0]].set(low).at[spots[1]].set(high)


def level_of(own_key, extent, cuts, low, largest):
    loudness, own = 1.0, jax.random.fold_in(own_key, 6)
    for position, blocks in cuts:
        draws = jnp.exp(jax.random.uniform(jax.random.fold_in(own, position), (blocks,), jnp.float32, low / len(cuts), largest / len(cuts)))
        loudness = loudness * jnp.repeat(draws, extent[position] // blocks).reshape([-1 if axis == position else 1 for axis in range(len(extent))])
    return loudness


def bell_draw(stream_key, dims, width, most, shards=(), kind=jnp.bfloat16):
    loudness = level_of(stream_key, dims, shards, -0.22, 0.18) if shards else 1.0
    drawn = jax.random.normal(stream_key, dims, jnp.float32) * width * loudness
    return jnp.minimum(jnp.maximum(drawn, -most), most).astype(kind)


def setup_inputs(seed: int = 0) -> dict:
    streams_of = jax.random.split(jax.random.key(seed), 8)
    density = bell_draw(streams_of[0], (X, Y, KX, KY), 1.0, 6.0, ((0, 32), (2, 8)), jnp.float32)
    potential_x = bell_draw(streams_of[1], (X, KX), 1.0, 6.0, ((0, 32),), jnp.float32)
    potential_y = bell_draw(streams_of[2], (Y, KY), 1.0, 6.0, (), jnp.float32)
    speeds_x = jnp.clip(jnp.exp(math.log(1.5) - 2.014903 * jax.random.uniform(streams_of[3], (KX,), jnp.float32) ** level_of(streams_of[3], (KX,), ((0, 8),), -0.2, 0.2)), 0.2, 1.5)
    speeds_y = jnp.clip(jnp.exp(jax.random.uniform(streams_of[4], (KY,), jnp.float32, math.log(0.2), math.log(1.5))), 0.2, 1.5)
    upwind_x = place_ends(jax.random.randint(streams_of[5], (KX,), 0, 2), jax.random.fold_in(streams_of[5], 1), 0, 1).astype(jnp.int32)
    upwind_y = place_ends(jax.random.randint(streams_of[6], (KY,), 0, 2), jax.random.fold_in(streams_of[6], 1), 0, 1).astype(jnp.int32)
    return dict(density=density, potential_x=potential_x, potential_y=potential_y, speeds_x=speeds_x, speeds_y=speeds_y, upwind_x=upwind_x, upwind_y=upwind_y)


step_size = 0.25


def tables(count):
    index = jnp.arange(count, dtype=jnp.int32)
    product = (index[:, None] * index[None, :]) % count
    angle = product.astype(jnp.float32) * (2.0 * math.pi / count)
    cosine = jnp.cos(angle)
    sine = jnp.sin(angle)
    forward = jnp.concatenate([cosine, sine], 0)
    backward = jnp.concatenate([sine, -cosine], 0) / count
    return forward, backward


def wigner_first(field, potential, forward, backward):
    hatted = jnp.einsum('ak,xykq->xyaq', forward, field, precision=lax.Precision.HIGHEST)
    weight = jnp.concatenate([potential, potential], 1)
    hatted = hatted * weight[:, None, :, None]
    return jnp.einsum('ak,xyaq->xykq', backward, hatted, precision=lax.Precision.HIGHEST)


def wigner_second(field, potential, forward, backward):
    hatted = jnp.einsum('aq,xykq->xyka', forward, field, precision=lax.Precision.HIGHEST)
    weight = jnp.concatenate([potential, potential], 1)
    hatted = hatted * weight[None, :, None, :]
    return jnp.einsum('aq,xyka->xykq', backward, hatted, precision=lax.Precision.HIGHEST)


def upwind(center, lower_two, lower_one, upper_one, upper_two, velocity):
    toward = velocity > 0
    first = jnp.where(toward, lower_one, upper_one)
    second = jnp.where(toward, lower_two, upper_two)
    return -jnp.abs(velocity) * (3.0 * center - 4.0 * first + second) * 0.5


def operator(field, potential_x, potential_y, vel_x, vel_y, tabs_x, tabs_y):
    padded = jnp.pad(field, ((2, 2), (2, 2), (0, 0), (0, 0)))
    center = padded[2:-2, 2:-2]
    along_x = upwind(center, padded[0:-4, 2:-2], padded[1:-3, 2:-2], padded[3:-1, 2:-2], padded[4:, 2:-2], vel_x[None, None, :, None])
    along_y = upwind(center, padded[2:-2, 0:-4], padded[2:-2, 1:-3], padded[2:-2, 3:-1], padded[2:-2, 4:], vel_y[None, None, None, :])

    def one_row(pair):
        row, prow = pair
        first = wigner_first(row[None], prow[None], tabs_x[0], tabs_x[1])
        second = wigner_second(row[None], potential_y, tabs_y[0], tabs_y[1])
        return (first + second)[0]

    theta = lax.map(one_row, (field, potential_x))
    return along_x + along_y + theta


def reference(density, potential_x, potential_y, speeds_x, speeds_y, upwind_x, upwind_y):
    vel_x = (2 * upwind_x - 1).astype(jnp.float32) * speeds_x
    vel_y = (2 * upwind_y - 1).astype(jnp.float32) * speeds_y
    tabs_x = tables(KX)
    tabs_y = tables(KY)
    section = density + step_size * operator(density, potential_x, potential_y, vel_x, vel_y, tabs_x, tabs_y)
    later = operator(section, potential_x, potential_y, vel_x, vel_y, tabs_x, tabs_y)
    return 0.5 * (density + section + step_size * later)
```

```python
import functools
import math

import jax
import jax.numpy as jnp
import numpy as np
from jax import lax
from jax.experimental import pallas as pl
from jax.experimental.pallas import tpu as pltpu
from jax.sharding import PartitionSpec as P


F32 = jnp.float32
BF16 = jnp.bfloat16
K = 128
AXES = ("gx", "ka")
SLOTS = [(dy, ds) for dy in (0, 2, 1, 3) for ds in (0, 1)]
VMEM = pl.BlockSpec(memory_space=pltpu.VMEM)
SMEM = pl.BlockSpec(memory_space=pltpu.SMEM)


def flat(x, y, z, core):
    return ((x * 4 + z % 4) * 2 + core) * 8 + y * 2 + z // 4


def place(block, part):
    x, low, core = block // 8, block // 2 % 4, block % 2
    half = part // 4
    y = part if half == 0 else 7 - part
    z = (low + 2 if x % 2 == 0 else 5 - low) + 4 * half
    return flat(x, y, z % 8, core)


def part_of(y, half):
    return y if half == 0 else 7 - y


def slot_part(ka, slot):
    dy, ds = SLOTS[slot]
    return part_of((ka // 2 + dy) % 4, (ka % 2) ^ ds)


def host_tables():
    table = np.zeros((256, 24), np.int32)
    for block in range(32):
        for ka in range(8):
            me = block * 8 + ka
            for slot in range(8):
                part = slot_part(ka, slot)
                table[me, slot] = part
                table[place(block, part), 8 + slot] = ka
            host = place(block, ka)
            table[host, 16] = block
            table[host, 17] = ka
    return table


def exchange_pairs(slot):
    return [
        (block * 8 + ka, place(block, slot_part(ka, slot)))
        for block in range(32)
        for ka in range(8)
    ]


def x_pairs(step):
    return [
        (place(block, part), place(block + step, part))
        for block in range(32)
        for part in range(8)
        if 0 <= block + step < 32
    ]


def y_pairs(step):
    return [
        (place(block, part), place(block, part + step))
        for block in range(32)
        for part in range(8)
        if 0 <= part + step < 8 and part // 4 == (part + step) // 4
    ]


def edge_pairs(y):
    return [
        (place(block, part_of(3, half)), place(block, part_of(y, half)))
        for block in range(32)
        for half in range(2)
    ]


def send(value, pairs):
    return lax.ppermute(value, AXES, pairs)


def halves(value):
    high = value.astype(BF16)
    return high, (value - high.astype(F32)).astype(BF16)


def circulant(row):
    return pltpu.roll(jnp.broadcast_to(row, (K, K)), 0, 1, stride=1, stride_axis=0)


def right_table(row):
    high, low = halves(circulant(row))
    return jnp.concatenate(
        [
            jnp.concatenate([high, low], 1),
            jnp.concatenate([high, jnp.zeros_like(low)], 1),
        ],
        0,
    )


def left_table(row):
    high, low = halves(circulant(row))
    return jnp.concatenate(
        [
            jnp.concatenate([high, high], 1),
            jnp.concatenate([low, jnp.zeros_like(low)], 1),
        ],
        0,
    )


def times_right(rows, table):
    both = jnp.dot(jnp.concatenate(halves(rows), 1), table, preferred_element_type=F32)
    return both[:, :K] + both[:, K:]


def times_left(table, first, second):
    high_0, low_0 = halves(first)
    high_1, low_1 = halves(second)
    stacked = jnp.concatenate(
        [jnp.concatenate([high_0, high_1], 1), jnp.concatenate([low_0, low_1], 1)], 0
    )
    both = jnp.dot(table, stacked, preferred_element_type=F32)
    both = both[:K] + both[K:]
    return both[:, :K], both[:, K:]


def slope(center, one, two):
    return 3.0 * center - 4.0 * one + two


def local_kernel(g_ref, ty_ref, vy_ref, out_ref, pad):
    vy = vy_ref[...].reshape(1, 1, K)
    toward = jnp.broadcast_to(vy > 0, (4, 16, K))
    rate = jnp.abs(vy) * 0.125

    def rows(ref, y):
        return ref[:, y]

    def step(value, one_low, two_low, one_high, two_high, table):
        one = jnp.where(toward, one_low, one_high)
        two = jnp.where(toward, two_low, two_high)
        wigner = times_right(value.reshape(64, K), table).reshape(4, 16, K)
        return wigner - rate * slope(value, one, two)

    edge = jnp.zeros((4, 2, 16, K), F32)
    pad[0, :, 0:2] = edge
    pad[0, :, 66:68] = edge
    pad[1, :, 0:2] = edge
    pad[1, :, 66:68] = edge
    for y in range(64):
        pad[0, :, y + 2] = g_ref[:, y]

    def turn(source, into):
        @pl.loop(0, 8)
        def _(group):
            block = ty_ref[pl.ds(pl.multiple_of(group * 8, 8), 8), :]
            for inner in range(8):
                y = group * 8 + inner
                value = pad[source, :, y + 2]
                moved = step(
                    value,
                    pad[source, :, y + 1],
                    pad[source, :, y],
                    pad[source, :, y + 3],
                    pad[source, :, y + 4],
                    right_table(block[inner : inner + 1]),
                )
                into(y, value, moved)

    def first(y, value, moved):
        pad[1, :, y + 2] = value + moved

    def second(y, value, moved):
        out_ref[:, y] = 0.5 * (pad[0, :, y + 2] + value + moved)

    turn(0, first)
    turn(1, second)


def gather_kernel(info_ref, *refs):
    pieces, (head_ref, tail_ref) = refs[:8], refs[8:]
    for slot in range(8):
        at = pl.ds(pl.multiple_of(info_ref[0, 8 + slot] * 16, 16), 16)
        head_ref[:, :, at, :] = pieces[slot][0:2]
        tail_ref[:, :, at, :] = pieces[slot][2:4]


def first_kernel(
    info_ref, head_ref, tail_ref, low_ref, high_ref, tx_ref, vx_ref, vy_ref,
    u_head_ref, u_tail_ref, y_low_ref, y_high_ref, e0_ref, e1_ref, e2_ref, e3_ref, tables,
):
    layers = [low_ref.at[0], low_ref.at[1], head_ref.at[0], head_ref.at[1], tail_ref.at[0], tail_ref.at[1], high_ref.at[0], high_ref.at[1]]
    outs = [u_head_ref.at[0], u_head_ref.at[1], u_tail_ref.at[0], u_tail_ref.at[1]]
    for x in range(4):
        tables[x] = left_table(tx_ref[x : x + 1, :])

    @pl.loop(0, 4)
    def _(pair):
        vx = vx_ref[...]
        toward = vx > 0
        rate = jnp.abs(vx) * 0.125
        for x in range(4):
            mine = [layers[x + 2][pair * 2 + i] for i in range(2)]
            wigner = times_left(tables[x], mine[0], mine[1])
            for i in range(2):
                y = pair * 2 + i
                one = jnp.where(toward, layers[x + 1][y], layers[x + 3][y])
                two = jnp.where(toward, layers[x][y], layers[x + 4][y])
                outs[x][y] = wigner[i] - rate * slope(mine[i], one, two)

    vy = vy_ref[...]
    upper = info_ref[0, 17] == 3
    keep = jnp.logical_or(
        jnp.logical_and(vy > 0, upper), jnp.logical_and(vy <= 0, jnp.logical_not(upper))
    )
    weight = jnp.where(keep, jnp.abs(vy) * -0.125, 0.0)
    for x in range(4):
        y_low_ref[x] = outs[x][0:2]
        y_high_ref[x] = outs[x][6:8]
        for part, ref in enumerate((e0_ref, e1_ref, e2_ref, e3_ref)):
            at = slice(32 * part, 32 * part + 32)
            near = jnp.where(upper, outs[x][7, at], outs[x][0, at])
            far = jnp.where(upper, outs[x][6, at], outs[x][1, at])
            one = weight * (far - 4.0 * near)
            two = weight * near
            ref[x, 0] = jnp.where(upper, one, two)
            ref[x, 1] = jnp.where(upper, two, one)


def second_kernel(
    info_ref, u_head_ref, u_tail_ref, low_ref, high_ref, y_low_ref, y_high_ref,
    e0_ref, e1_ref, e2_ref, e3_ref, tx_ref, ty_ref, vx_ref, vy_ref, *refs,
):
    pieces, (result, tables) = refs[:8], refs[8:]
    layers = [low_ref.at[0], low_ref.at[1], u_head_ref.at[0], u_head_ref.at[1], u_tail_ref.at[0], u_tail_ref.at[1], high_ref.at[0], high_ref.at[1]]
    for x in range(4):
        tables[x] = left_table(0.5 * tx_ref[x : x + 1, :])

    def row(x, y):
        if y < 0:
            return y_low_ref[x, y + 2]
        if y > 7:
            return y_high_ref[x, y - 8]
        return layers[x + 2][y]

    vx = vx_ref[...]
    toward = vx > 0
    rate = jnp.abs(vx) * 0.0625
    vy = jnp.broadcast_to(vy_ref[...], (K, K))
    toward_y = vy > 0
    rate_y = jnp.abs(vy) * 0.125
    for pair in range(4):
        right = [right_table(ty_ref[pair * 2 + i : pair * 2 + i + 1, :]) for i in range(2)]
        for x in range(4):
            mine = [layers[x + 2][pair * 2 + i] for i in range(2)]
            wigner = times_left(tables[x], mine[0], mine[1])
            for i in range(2):
                y = pair * 2 + i
                one = jnp.where(toward, layers[x + 1][y], layers[x + 3][y])
                two = jnp.where(toward, layers[x][y], layers[x + 4][y])
                total = mine[i] + wigner[i] - rate * slope(mine[i], one, two)
                total += times_right(mine[i], right[i])
                one = jnp.where(toward_y, row(x, y - 1), row(x, y + 1))
                two = jnp.where(toward_y, row(x, y - 2), row(x, y + 2))
                result[x, y] = total - rate_y * slope(mine[i], one, two)

    last = info_ref[0, 18] == 3
    half = info_ref[0, 19]
    for slot, (dy, ds) in enumerate(SLOTS):
        at = pl.ds(pl.multiple_of(info_ref[0, 8 + slot] * 16, 16), 16)
        pieces[slot][:, 0:8] = result[:, :, at, :]
        if dy == 0:
            at = pl.ds(pl.multiple_of((half ^ ds) * 16, 16), 16)
            own = jnp.where(last, e3_ref[:, :, at, :], 0.0)
            others = e0_ref[:, :, at, :] + e1_ref[:, :, at, :] + e2_ref[:, :, at, :]
            pieces[slot][:, 8:10] = own + others


def final_kernel(info_ref, local_ref, *refs):
    pieces, out_ref = refs[:8], refs[8]
    for slot, (dy, ds) in enumerate(SLOTS):
        at = pl.ds(pl.multiple_of(info_ref[0, slot] * 8, 8), 8)
        out_ref[:, at] = local_ref[:, at] + pieces[slot][:, 0:8]
    for slot, (dy, ds) in enumerate(SLOTS):
        if dy == 0:
            half = info_ref[0, 20] ^ ds
            at = pl.ds(jnp.where(half == 0, 32, 30), 2)
            out_ref[:, at] = out_ref[:, at] + pieces[slot][:, 8:10]


def cost(flops, size):
    return pl.CostEstimate(flops=flops, bytes_accessed=size, transcendentals=0)


PARAMS = pltpu.CompilerParams(vmem_limit_bytes=40 * 1024 * 1024)
MIB = 1 << 20


def array(*shape):
    return jax.ShapeDtypeStruct(shape, F32)


def sine_table(sign):
    index = np.arange(K)
    angle = (sign * index[:, None] * index[None, :] % K) * (2.0 * math.pi / K)
    return (np.sin(angle) / K).astype(np.float32)


def per_device(table, density, potential_x, potential_y, speeds_x, speeds_y, upwind_x, upwind_y):
    me = lax.axis_index("gx") * 8 + lax.axis_index("ka")
    info = lax.dynamic_slice(jnp.asarray(table), (me, 0), (1, table.shape[1]))

    pieces = []
    for slot in range(8):
        start = info[0, slot] * 8
        piece = lax.dynamic_slice(density, (0, start, 0, 0), (4, 8, 16, K))
        pieces.append(send(piece, exchange_pairs(slot)))
    moved_x = send(potential_x, exchange_pairs(0))
    vel_x = lax.all_gather((2 * upwind_x - 1).astype(F32) * speeds_x, "ka", tiled=True)
    vx = jnp.broadcast_to(vel_x[:, None], (K, K))
    vy = ((2 * upwind_y - 1).astype(F32) * speeds_y).reshape(1, K)

    highest = lax.Precision.HIGHEST
    ty = 0.25 * jnp.dot(potential_y, jnp.asarray(sine_table(1)), precision=highest)
    tx = 0.25 * jnp.dot(moved_x, jnp.asarray(sine_table(-1)), precision=highest)
    ty_own = lax.dynamic_slice(ty, (info[0, 17] * 8, 0), (8, K))

    local = pl.pallas_call(
        local_kernel,
        out_shape=array(4, 64, 16, K),
        in_specs=[VMEM] * 3,
        out_specs=VMEM,
        scratch_shapes=[pltpu.VMEM((2, 4, 68, 16, K), F32)],
        compiler_params=PARAMS,
        cost_estimate=cost(4 * 10**9, 4 * MIB),
        name="local_part",
    )(density, ty, vy)

    head, tail = pl.pallas_call(
        gather_kernel,
        out_shape=[array(2, 8, K, K)] * 2,
        in_specs=[SMEM] + [VMEM] * 8,
        out_specs=[VMEM] * 2,
        compiler_params=PARAMS,
        cost_estimate=cost(0, 4 * MIB),
        name="gather_kx",
    )(info, *pieces)
    low = send(tail, x_pairs(1))
    high = send(head, x_pairs(-1))

    u_head, u_tail, y_low, y_high, *edges = pl.pallas_call(
        first_kernel,
        out_shape=[array(2, 8, K, K)] * 2 + [array(4, 2, K, K)] * 2 + [array(4, 2, 32, K)] * 4,
        in_specs=[SMEM] + [VMEM] * 7,
        out_specs=[VMEM] * 8,
        scratch_shapes=[pltpu.VMEM((4, 2 * K, 2 * K), BF16)],
        compiler_params=PARAMS,
        cost_estimate=cost(10**9, 8 * MIB),
        name="first_turn",
    )(info, head, tail, low, high, tx, vx, vy)
    low = send(u_tail, x_pairs(1))
    high = send(u_head, x_pairs(-1))
    y_under = send(y_high, y_pairs(1))
    y_over = send(y_low, y_pairs(-1))
    edges = [send(edges[y], edge_pairs(y)) for y in range(3)] + [edges[3]]

    back = pl.pallas_call(
        second_kernel,
        out_shape=[array(4, 10 if dy == 0 else 8, 16, K) for dy, ds in SLOTS],
        in_specs=[SMEM] + [VMEM] * 14,
        out_specs=[VMEM] * 8,
        scratch_shapes=[pltpu.VMEM((4, 8, K, K), F32), pltpu.VMEM((4, 2 * K, 2 * K), BF16)],
        compiler_params=PARAMS,
        cost_estimate=cost(2 * 10**9, 10 * MIB),
        name="second_turn",
    )(info, u_head, u_tail, low, high, y_under, y_over, *edges, tx, ty_own, vx, vy)
    pieces = [
        send(back[slot], [(there, here) for here, there in exchange_pairs(slot)])
        for slot in range(8)
    ]

    return pl.pallas_call(
        final_kernel,
        grid=(4,),
        out_shape=array(4, 64, 16, K),
        in_specs=[SMEM, pl.BlockSpec((1, 64, 16, K), lambda x: (x, 0, 0, 0))]
        + [
            pl.BlockSpec((1, 10 if dy == 0 else 8, 16, K), lambda x: (x, 0, 0, 0))
            for dy, ds in SLOTS
        ],
        out_specs=pl.BlockSpec((1, 64, 16, K), lambda x: (x, 0, 0, 0)),
        compiler_params=PARAMS,
        cost_estimate=cost(0, 6 * MIB),
        name="add_back",
    )(info, local, *pieces)


def solution(mesh):
    table = host_tables()
    for block in range(32):
        for part in range(8):
            host = place(block, part)
            table[host, 18] = part if part < 4 else 7 - part
            table[host, 19] = part // 4
            table[block * 8 + part, 20] = part % 2
    in_specs = (P("gx", None, "ka", None), P("gx", None), P(), P("ka"), P(), P("ka"), P())
    out_specs = P("gx", None, "ka", None)
    return jax.shard_map(
        functools.partial(per_device, table),
        mesh=mesh,
        in_specs=in_specs,
        out_specs=out_specs,
        check_vma=False,
    )
```

```python
import math

import jax
import jax.numpy as jnp
import numpy as np
from jax import lax
from jax.experimental import pallas as pl
from jax.experimental.pallas import tpu as pltpu
from jax.sharding import PartitionSpec as P


F32 = jnp.float32
BF16 = jnp.bfloat16
K = 128
AXES = ("gx", "ka")
SLOTS = [(dy, ds) for dy in (0, 2, 1, 3) for ds in (0, 1)]
VMEM = pl.BlockSpec(memory_space=pltpu.VMEM)


def flat(x, y, z, core):
    return ((x * 4 + z % 4) * 2 + core) * 8 + y * 2 + z // 4


def place(block, part):
    x, low, core = block // 8, block // 2 % 4, block % 2
    half = part // 4
    y = part if half == 0 else 7 - part
    z = (low + 2 if x % 2 == 0 else 5 - low) + 4 * half
    return flat(x, y, z % 8, core)


def part_of(y, half):
    return y if half == 0 else 7 - y


def slot_part(ka, slot):
    dy, ds = SLOTS[slot]
    return part_of((ka // 2 + dy) % 4, (ka % 2) ^ ds)


def exchange_pairs(slot):
    return [
        (block * 8 + ka, place(block, slot_part(ka, slot)))
        for block in range(32)
        for ka in range(8)
    ]


def x_pairs(step):
    return [
        (place(block, part), place(block + step, part))
        for block in range(32)
        for part in range(8)
        if 0 <= block + step < 32
    ]


def y_pairs(step):
    return [
        (place(block, part), place(block, part + step))
        for block in range(32)
        for part in range(8)
        if 0 <= part + step < 8 and part // 4 == (part + step) // 4
    ] + [
        (place(block, part), place(block, part_of(0, part // 4)))
        for block in range(32)
        for part in [3 if step == 1 else 4]
    ]


def edge_pairs():
    return [
        (place(block, part_of(3, half)), place(block, part_of(1, half)))
        for block in range(32)
        for half in range(2)
    ]


def send(value, pairs):
    return lax.ppermute(value, AXES, pairs)


def as_source():
    ka = lax.axis_index("ka")
    return ka >> 1, ka & 1


def as_host():
    gx, ka = lax.axis_index("gx"), lax.axis_index("ka")
    z = (ka & 1) * 4 + ((gx >> 1) & 3)
    turn = jnp.where(((gx >> 3) & 1) == 0, z - 2, 5 - z) & 7
    return ka >> 1, turn >> 2


def part_index(y, half):
    return y + half * (7 - 2 * y)


def rows_to(slot):
    y, half = as_source()
    dy, ds = SLOTS[slot]
    return pl.ds(pl.multiple_of(part_index((y + dy) & 3, half ^ ds) * 8, 8), 8)


def kx_of(slot):
    y, half = as_host()
    dy, ds = SLOTS[slot]
    return pl.ds(pl.multiple_of((((y - dy) & 3) * 2 + (half ^ ds)) * 16, 16), 16)


def halves(value):
    high = value.astype(BF16)
    return high, (value - high.astype(F32)).astype(BF16)


def circulant(row):
    return pltpu.roll(jnp.broadcast_to(row, (K, K)), 0, 1, stride=1, stride_axis=0)


def right_table(row):
    high, low = halves(circulant(row))
    return jnp.concatenate(
        [
            jnp.concatenate([high, low], 1),
            jnp.concatenate([high, jnp.zeros_like(low)], 1),
        ],
        0,
    )


def left_table(row):
    high, low = halves(circulant(row))
    return jnp.concatenate(
        [
            jnp.concatenate([high, high], 1),
            jnp.concatenate([low, jnp.zeros_like(low)], 1),
        ],
        0,
    )


def times_right(rows, table):
    both = jnp.dot(jnp.concatenate(halves(rows), 1), table, preferred_element_type=F32)
    return both[:, :K] + both[:, K:]


def times_left(table, first, second):
    high_0, low_0 = halves(first)
    high_1, low_1 = halves(second)
    stacked = jnp.concatenate(
        [jnp.concatenate([high_0, high_1], 1), jnp.concatenate([low_0, low_1], 1)], 0
    )
    both = jnp.dot(table, stacked, preferred_element_type=F32)
    both = both[:K] + both[K:]
    return both[:, :K], both[:, K:]


def slope(center, one, two):
    return 3.0 * center - 4.0 * one + two


def local_kernel(g_ref, ty_ref, vy_ref, out_ref, pad):
    vy = vy_ref[...].reshape(1, 1, K)
    toward = jnp.broadcast_to(vy > 0, (4, 16, K))
    rate = jnp.abs(vy) * 0.125

    def step(value, one_low, two_low, one_high, two_high, table):
        one = jnp.where(toward, one_low, one_high)
        two = jnp.where(toward, two_low, two_high)
        wigner = times_right(value.reshape(64, K), table).reshape(4, 16, K)
        return wigner - rate * slope(value, one, two)

    edge = jnp.zeros((4, 2, 16, K), F32)
    pad[0, :, 0:2] = edge
    pad[0, :, 66:68] = edge
    pad[1, :, 0:2] = edge
    pad[1, :, 66:68] = edge
    for y in range(64):
        pad[0, :, y + 2] = g_ref[:, y]

    def turn(source, into):
        @pl.loop(0, 8)
        def _(group):
            block = ty_ref[pl.ds(pl.multiple_of(group * 8, 8), 8), :]
            for inner in range(8):
                y = group * 8 + inner
                value = pad[source, :, y + 2]
                moved = step(
                    value,
                    pad[source, :, y + 1],
                    pad[source, :, y],
                    pad[source, :, y + 3],
                    pad[source, :, y + 4],
                    right_table(block[inner : inner + 1]),
                )
                into(y, value, moved)

    def first(y, value, moved):
        pad[1, :, y + 2] = value + moved

    def second(y, value, moved):
        out_ref[:, y] = 0.5 * (pad[0, :, y + 2] + value + moved)

    turn(0, first)
    turn(1, second)


def pack_kernel(g_ref, vel_ref, potential_ref, *pieces):
    for slot in range(8):
        at = rows_to(slot)
        for x in range(4):
            pieces[slot][8 * x : 8 * x + 8] = g_ref[x, at]
        pieces[slot][32] = vel_ref[...]
    pieces[0][33, 0:4] = potential_ref[...]
    pieces[0][33, 4:16] = jnp.zeros((12, K), F32)


def cut_kernel(*refs):
    pieces, (head_ref, tail_ref) = refs[:4], refs[4:]
    for i in range(4):
        head_ref[i] = pieces[i][0:16]
        tail_ref[i] = pieces[i][16:32]


def inner_drift(center, x, layer, toward, rate):
    total = 3.0 * center
    for step, factor in ((1, -4.0), (2, 1.0)):
        low = layer(x - step) if x - step >= 0 else None
        high = layer(x + step) if x + step <= 3 else None
        if low is None:
            if high is not None:
                total += factor * jnp.where(toward, 0.0, high)
        elif high is None:
            total += factor * jnp.where(toward, low, 0.0)
        else:
            total += factor * jnp.where(toward, low, high)
    return -rate * total


def first_kernel(*refs):
    pieces, sine_ref, (u_ref, vx_ref, tx_ref), (field, tables) = refs[:8], refs[8], refs[9:12], refs[12:]
    for slot in range(8):
        at = kx_of(slot)
        for x in range(4):
            field[x, :, at, :] = pieces[slot][8 * x : 8 * x + 8]
        vx_ref[at, :] = pieces[slot][32]
    tx_ref[...] = 0.25 * jnp.dot(
        pieces[0][33, 0:8], sine_ref[...], precision=lax.Precision.HIGHEST, preferred_element_type=F32
    )
    for x in range(4):
        tables[x] = left_table(tx_ref[x : x + 1, :])

    @pl.loop(0, 4)
    def _(pair):
        vx = vx_ref[...]
        toward = vx > 0
        rate = jnp.abs(vx) * 0.125
        for x in range(4):
            mine = [field[x, pair * 2 + i] for i in range(2)]
            wigner = times_left(tables[x], mine[0], mine[1])
            for i in range(2):
                y = pair * 2 + i
                u_ref[x, y] = wigner[i] + inner_drift(mine[i], x, lambda at: field[at, y], toward, rate)


def first_edge_kernel(
    inner_ref, low_a_ref, low_b_ref, high_a_ref, high_b_ref, vx_ref, vy_ref,
    u_head_ref, u_tail_ref, y_low_ref, y_high_ref, edge_ref, own_edge_ref,
):
    for slot in range(8):
        at = kx_of(slot)
        low = (low_a_ref if slot < 4 else low_b_ref).at[slot % 4]
        high = (high_a_ref if slot < 4 else high_b_ref).at[slot % 4]
        vx = vx_ref[at, :]
        up = (jnp.maximum(vx, 0.0) * 0.125)[None]
        down = (jnp.maximum(-vx, 0.0) * 0.125)[None]
        near = low[8:16]
        u_head_ref[0, :, at, :] = inner_ref[0, :, at, :] + up * (4.0 * near - low[0:8])
        u_head_ref[1, :, at, :] = inner_ref[1, :, at, :] - up * near
        near = high[0:8]
        u_tail_ref[0, :, at, :] = inner_ref[2, :, at, :] - down * near
        u_tail_ref[1, :, at, :] = inner_ref[3, :, at, :] + down * (4.0 * near - high[8:16])

    vy = vy_ref[...]
    y_place, half = as_host()
    upper = half == 0
    last = y_place == 3
    keep = jnp.logical_or(
        jnp.logical_and(vy > 0, upper), jnp.logical_and(vy <= 0, jnp.logical_not(upper))
    )
    weight = jnp.where(keep, jnp.abs(vy) * -0.125, 0.0)
    for x in range(4):
        u = u_head_ref.at[x] if x < 2 else u_tail_ref.at[x - 2]
        y_low_ref[x, :, 0:K] = jnp.where(jnp.logical_and(last, jnp.logical_not(upper)), 0.0, u[0:2])
        y_high_ref[x, :, 0:K] = jnp.where(jnp.logical_and(last, upper), 0.0, u[6:8])
        parts = []
        for part in range(4):
            at = slice(32 * part, 32 * part + 32)
            near = jnp.where(upper, u[7, at], u[0, at])
            far = jnp.where(upper, u[6, at], u[1, at])
            one = weight * (far - 4.0 * near)
            two = weight * near
            parts.append((jnp.where(upper, one, two), jnp.where(upper, two, one)))
        for row in range(2):
            y_low_ref[x, row, K : K + 32] = jnp.where(upper, parts[2][row], parts[0][row])
            y_high_ref[x, row, K : K + 32] = jnp.where(upper, parts[0][row], parts[2][row])
            edge_ref[x, row] = parts[1][row]
            own_edge_ref[x, row] = parts[3][row]


def second_kernel(u_head_ref, u_tail_ref, tx_ref, ty_ref, vx_ref, vy_ref, out_ref, tables):
    layers = [u_head_ref.at[0], u_head_ref.at[1], u_tail_ref.at[0], u_tail_ref.at[1]]
    for x in range(4):
        tables[x] = left_table(0.5 * tx_ref[x : x + 1, :])
    y_place, half = as_host()
    ty = ty_ref[pl.ds(pl.multiple_of(part_index(y_place, half) * 8, 8), 8), :]

    vx = vx_ref[...]
    toward = vx > 0
    rate = jnp.abs(vx) * 0.0625
    vy = jnp.broadcast_to(vy_ref[...], (K, K))
    toward_y = vy > 0
    rate_y = jnp.abs(vy) * 0.125
    zero = jnp.zeros((K, K), F32)
    for pair in range(4):
        right = [right_table(ty[pair * 2 + i : pair * 2 + i + 1, :]) for i in range(2)]
        for x in range(4):
            mine = [layers[x][pair * 2 + i] for i in range(2)]
            wigner = times_left(tables[x], mine[0], mine[1])
            for i in range(2):
                y = pair * 2 + i
                total = mine[i] + wigner[i]
                total += inner_drift(mine[i], x, lambda at: layers[at][y], toward, rate)
                total += times_right(mine[i], right[i])
                near = [layers[x][at] if 0 <= at < 8 else zero for at in (y - 2, y - 1, y + 1, y + 2)]
                one = jnp.where(toward_y, near[1], near[2])
                two = jnp.where(toward_y, near[0], near[3])
                out_ref[x, y] = total - rate_y * slope(mine[i], one, two)


def second_edge_kernel(
    inner_ref, low_ref, high_ref, y_low_ref, y_high_ref, edge_ref, own_edge_ref, vx_ref, vy_ref, *pieces
):
    vy = vy_ref[...].reshape(1, 1, K)
    up_y = jnp.maximum(vy, 0.0) * 0.125
    down_y = jnp.maximum(-vy, 0.0) * 0.125

    def total(at, x):
        vx = vx_ref[at, :]
        up = (jnp.maximum(vx, 0.0) * 0.0625)[None]
        down = (jnp.maximum(-vx, 0.0) * 0.0625)[None]
        value = inner_ref[x, :, at, :]
        if x == 0:
            value += up * (4.0 * low_ref[1, :, at, :] - low_ref[0, :, at, :])
        if x == 1:
            value -= up * low_ref[1, :, at, :]
        if x == 2:
            value -= down * high_ref[0, :, at, :]
        if x == 3:
            value += down * (4.0 * high_ref[0, :, at, :] - high_ref[1, :, at, :])
        near, far = y_low_ref[x, 1:2, at, :], y_low_ref[x, 0:1, at, :]
        rows = [up_y * (4.0 * near - far), -up_y * near]
        near, far = y_high_ref[x, 0:1, at, :], y_high_ref[x, 1:2, at, :]
        rows += [-down_y * near, down_y * (4.0 * near - far)]
        return value, rows

    for slot in range(8):
        at = kx_of(slot)
        for x in range(4):
            value, rows = total(at, x)
            pieces[slot][x, 0:2] = value[0:2] + jnp.concatenate(rows[:2], 0)
            pieces[slot][x, 2:6] = value[2:6]
            pieces[slot][x, 6:8] = value[6:8] + jnp.concatenate(rows[2:], 0)

    y_place, half = as_host()
    ends = jnp.logical_or(y_place == 0, y_place == 2)
    under = jnp.logical_and(ends, (y_place == 0) == (half == 0))
    for slot in range(2):
        at = pl.multiple_of((half ^ SLOTS[slot][1]) * 16, 16)
        with_rows = pl.ds(pl.multiple_of(K + at, 16), 16)
        at = pl.ds(at, 16)
        for x in range(4):
            alone = jnp.where(y_place == 3, own_edge_ref[x, :, at, :], edge_ref[x, :, at, :])
            paired = jnp.where(under, y_low_ref[x, :, with_rows, :], y_high_ref[x, :, with_rows, :])
            pieces[slot][x, 8:10] = jnp.where(ends, paired, alone)


def final_kernel(local_ref, *refs):
    pieces, out_ref = refs[:8], refs[8]
    for slot in range(8):
        at = rows_to(slot)
        out_ref[:, at] = local_ref[:, at] + pieces[slot][:, 0:8]
    for slot in range(2):
        half = as_source()[1] ^ SLOTS[slot][1]
        at = pl.ds(32 - 2 * half, 2)
        out_ref[:, at] = out_ref[:, at] + pieces[slot][:, 8:10]


MIB = 1 << 20


def array(*shape):
    return jax.ShapeDtypeStruct(shape, F32)


def params():
    return pltpu.CompilerParams(vmem_limit_bytes=40 * MIB)


def cost(flops, mib):
    return pl.CostEstimate(flops=flops, bytes_accessed=mib * MIB, transcendentals=0)


def call(kernel, outs, scratch=(), flops=0, mib=4):
    def run(*operands):
        return pl.pallas_call(
            kernel,
            out_shape=outs,
            in_specs=[VMEM] * len(operands),
            out_specs=[VMEM] * len(outs) if isinstance(outs, list) else VMEM,
            scratch_shapes=list(scratch),
            compiler_params=params(),
            cost_estimate=cost(flops, mib),
            name=kernel.__name__,
        )(*operands)

    return run


def sine_table(sign):
    index = np.arange(K)
    angle = (sign * index[:, None] * index[None, :] % K) * (2.0 * math.pi / K)
    return (np.sin(angle) / K).astype(np.float32)


def back(pairs):
    return [(there, here) for here, there in pairs]


def per_device(density, potential_x, potential_y, speeds_x, speeds_y, upwind_x, upwind_y):
    vel_x = (2 * upwind_x - 1).astype(F32) * speeds_x
    vel_x = jnp.broadcast_to(vel_x[:, None], (16, K))
    vy = ((2 * upwind_y - 1).astype(F32) * speeds_y).reshape(1, K)

    pieces = call(pack_kernel, [array(34, 16, K)] + [array(33, 16, K)] * 7)(density, vel_x, potential_x)
    pieces = [send(piece, exchange_pairs(slot)) for slot, piece in enumerate(pieces)]

    highest = lax.Precision.HIGHEST
    ty = 0.25 * jnp.dot(potential_y, jnp.asarray(sine_table(1)), precision=highest)
    local = call(
        local_kernel, array(4, 64, 16, K), [pltpu.VMEM((2, 4, 68, 16, K), F32)], 4 * 10**9
    )(density, ty, vy)

    low, high = [], []
    for group in range(2):
        head, tail = call(cut_kernel, [array(4, 16, 16, K)] * 2, mib=2)(*pieces[4 * group : 4 * group + 4])
        low.append(send(tail, x_pairs(1)))
        high.append(send(head, x_pairs(-1)))
    left_tables = pltpu.VMEM((4, 2 * K, 2 * K), BF16)
    inner, vx, tx = call(
        first_kernel,
        [array(4, 8, K, K), array(K, K), array(8, K)],
        [pltpu.VMEM((4, 8, K, K), F32), left_tables],
        2 * 10**9,
    )(*pieces, jnp.asarray(sine_table(-1)))
    u_head, u_tail, y_low, y_high, edge, own_edge = call(
        first_edge_kernel,
        [array(2, 8, K, K)] * 2 + [array(4, 2, K + 32, K)] * 2 + [array(4, 2, 32, K)] * 2,
    )(inner, *low, *high, vx, vy)

    low = send(u_tail, x_pairs(1))
    high = send(u_head, x_pairs(-1))
    y_under = send(y_high, y_pairs(1))
    y_over = send(y_low, y_pairs(-1))
    edge = send(edge, edge_pairs())
    inner = call(second_kernel, array(4, 8, K, K), [left_tables], 3 * 10**9)(u_head, u_tail, tx, ty, vx, vy)
    pieces = call(second_edge_kernel, [array(4, 10, 16, K)] * 2 + [array(4, 8, 16, K)] * 6)(
        inner, low, high, y_under, y_over, edge, own_edge, vx, vy
    )
    pieces = [send(piece, back(exchange_pairs(slot))) for slot, piece in enumerate(pieces)]

    def by_x(*shape):
        return pl.BlockSpec((1, *shape), lambda x: (x, 0, 0, 0))

    return pl.pallas_call(
        final_kernel,
        grid=(4,),
        out_shape=array(4, 64, 16, K),
        in_specs=[by_x(64, 16, K)] + [by_x(10, 16, K)] * 2 + [by_x(8, 16, K)] * 6,
        out_specs=by_x(64, 16, K),
        compiler_params=params(),
        cost_estimate=cost(0, 6),
        name="final_kernel",
    )(local, *pieces)


def solution(mesh):
    in_specs = (P("gx", None, "ka", None), P("gx", None), P(), P("ka"), P(), P("ka"), P())
    out_specs = P("gx", None, "ka", None)
    return jax.shard_map(
        per_device, mesh=mesh, in_specs=in_specs, out_specs=out_specs, check_vma=False
    )
```

```python
import functools
import math

import jax
import jax.numpy as jnp
import numpy as np
from jax import lax
from jax.experimental import pallas as pl
from jax.experimental.pallas import tpu as pltpu
from jax.sharding import PartitionSpec as P


F32 = jnp.float32
BF16 = jnp.bfloat16
K = 128
AXES = ("gx", "ka")
SLOTS = [(dy, ds) for dy in (3, 0, 1, 2) for ds in (0, 1)]
GROUPS = (range(0, 2), range(2, 8))
FIRST = SLOTS.index((0, 0))
VMEM = pl.BlockSpec(memory_space=pltpu.VMEM)


def flat(x, y, z, core):
    return ((x * 4 + z % 4) * 2 + core) * 8 + y * 2 + z // 4


def place(block, part):
    x, low, core = block // 8, block // 2 % 4, block % 2
    half = part // 4
    y = part if half == 0 else 7 - part
    z = (low + 2 if x % 2 == 0 else 5 - low) + 4 * half
    return flat(x, y, z % 8, core)


def part_of(y, half):
    return y if half == 0 else 7 - y


def slot_part(ka, slot):
    dy, ds = SLOTS[slot]
    return part_of((ka // 2 + dy) % 4, (ka % 2) ^ ds)


def exchange_pairs(slot):
    return [
        (block * 8 + ka, place(block, slot_part(ka, slot)))
        for block in range(32)
        for ka in range(8)
    ]


def x_pairs(step):
    return [
        (place(block, part), place((block + step) % 32, part))
        for block in range(32)
        for part in range(8)
    ]


def y_pairs(step):
    return [
        (place(block, 4 * half + part), place(block, 4 * half + (part + step) % 4))
        for block in range(32)
        for half in range(2)
        for part in range(4)
    ]


def send(value, pairs):
    return lax.ppermute(value, AXES, pairs)


def as_source():
    ka = lax.axis_index("ka")
    return ka >> 1, ka & 1


def as_host():
    gx, ka = lax.axis_index("gx"), lax.axis_index("ka")
    z = (ka & 1) * 4 + ((gx >> 1) & 3)
    turn = jnp.where(((gx >> 3) & 1) == 0, z - 2, 5 - z) & 7
    return ka >> 1, turn >> 2, (gx & 25) + (turn & 3) * 2


def part_index(y, half):
    return y + half * (7 - 2 * y)


def rows_to(slot):
    y, half = as_source()
    dy, ds = SLOTS[slot]
    return pl.ds(pl.multiple_of(part_index((y + dy) & 3, half ^ ds) * 8, 8), 8)


def kx_of(slot):
    y, half, block = as_host()
    dy, ds = SLOTS[slot]
    return pl.ds(pl.multiple_of((((y - dy) & 3) * 2 + (half ^ ds)) * 16, 16), 16)


def halves(value):
    high = value.astype(BF16)
    return high, (value - high.astype(F32)).astype(BF16)


def circulant(row):
    return pltpu.roll(jnp.broadcast_to(row, (K, K)), 0, 1, stride=1, stride_axis=0)


def right_table(row):
    high, low = halves(circulant(row))
    return jnp.concatenate(
        [
            jnp.concatenate([high, low], 1),
            jnp.concatenate([high, jnp.zeros_like(low)], 1),
        ],
        0,
    )


def left_table(row):
    high, low = halves(circulant(row))
    return jnp.concatenate(
        [
            jnp.concatenate([high, high], 1),
            jnp.concatenate([low, jnp.zeros_like(low)], 1),
        ],
        0,
    )


def times_right(rows, table):
    both = jnp.dot(jnp.concatenate(halves(rows), 1), table, preferred_element_type=F32)
    return both[:, :K] + both[:, K:]


def times_left(table, first, second):
    high_0, low_0 = halves(first)
    high_1, low_1 = halves(second)
    stacked = jnp.concatenate(
        [jnp.concatenate([high_0, high_1], 1), jnp.concatenate([low_0, low_1], 1)], 0
    )
    both = jnp.dot(table, stacked, preferred_element_type=F32)
    both = both[:K] + both[K:]
    return both[:, :K], both[:, K:]


def slope(center, one, two):
    return 3.0 * center - 4.0 * one + two


def local_kernel(g_ref, ty_ref, vy_ref, out_ref, pad):
    vy = vy_ref[...].reshape(1, 1, K)
    toward = jnp.broadcast_to(vy > 0, (4, 16, K))
    rate = jnp.abs(vy) * 0.125

    def step(value, one_low, two_low, one_high, two_high, table):
        one = jnp.where(toward, one_low, one_high)
        two = jnp.where(toward, two_low, two_high)
        wigner = times_right(value.reshape(64, K), table).reshape(4, 16, K)
        return wigner - rate * slope(value, one, two)

    edge = jnp.zeros((4, 2, 16, K), F32)
    pad[0, :, 0:2] = edge
    pad[0, :, 66:68] = edge
    pad[1, :, 0:2] = edge
    pad[1, :, 66:68] = edge
    for y in range(64):
        pad[0, :, y + 2] = g_ref[:, y]

    def turn(source, into):
        @pl.loop(0, 8)
        def _(group):
            block = ty_ref[pl.ds(pl.multiple_of(group * 8, 8), 8), :]
            for inner in range(8):
                y = group * 8 + inner
                value = pad[source, :, y + 2]
                moved = step(
                    value,
                    pad[source, :, y + 1],
                    pad[source, :, y],
                    pad[source, :, y + 3],
                    pad[source, :, y + 4],
                    right_table(block[inner : inner + 1]),
                )
                into(y, value, moved)

    def first(y, value, moved):
        pad[1, :, y + 2] = value + moved

    def second(y, value, moved):
        out_ref[:, y] = 0.5 * (pad[0, :, y + 2] + value + moved)

    turn(0, first)
    turn(1, second)


def pack_kernel(g_ref, vel_ref, potential_ref, *pieces):
    y, half = as_source()
    for slot in range(8):
        at = rows_to(slot)
        for x in range(4):
            pieces[slot][8 * x : 8 * x + 8] = g_ref[x, at]
        pieces[slot][32] = vel_ref[...]
        dy, ds = SLOTS[slot]
        if dy == 0:
            at = pl.ds(32 - 2 * (half ^ ds), 2)
            for x in range(4):
                pieces[slot][33 + 2 * x : 35 + 2 * x] = g_ref[x, at]
    pieces[FIRST][41, 0:4] = potential_ref[...]
    pieces[FIRST][41, 4:16] = jnp.zeros((12, K), F32)


def cut_kernel(slots, *refs):
    pieces, outs = refs[: len(slots)], refs[len(slots) :]
    head_ref, tail_ref, y_low_ref, y_high_ref = outs[:4]
    for i, slot in enumerate(slots):
        head_ref[i] = pieces[i][0:16]
        tail_ref[i] = pieces[i][16:32]
        for x in range(4):
            y_low_ref[i, 2 * x : 2 * x + 2] = pieces[i][8 * x : 8 * x + 2]
            y_high_ref[i, 2 * x : 2 * x + 2] = pieces[i][8 * x + 6 : 8 * x + 8]
        dy, ds = SLOTS[slot]
        if dy == 0:
            rows = pieces[i][33:41]
            y_low_ref[len(slots) + ds] = rows
            y_high_ref[len(slots) + ds] = rows
            outs[4][ds] = rows


def inner_drift(center, x, layer, toward, rate):
    total = 3.0 * center
    for step, factor in ((1, -4.0), (2, 1.0)):
        low = layer(x - step) if x - step >= 0 else None
        high = layer(x + step) if x + step <= 3 else None
        if low is None:
            if high is not None:
                total += factor * jnp.where(toward, 0.0, high)
        elif high is None:
            total += factor * jnp.where(toward, low, 0.0)
        else:
            total += factor * jnp.where(toward, low, high)
    return -rate * total


def outer_drift(x, low, high, up, down):
    if x == 0:
        return up * (4.0 * low(0) - low(1))
    if x == 1:
        return -up * low(0)
    if x == 2:
        return -down * high(0)
    return down * (4.0 * high(0) - high(1))


def rates(vx_ref, at, factor):
    vx = vx_ref[at, :]
    block = as_host()[2]
    up = jnp.where(block == 0, 0.0, jnp.maximum(vx, 0.0) * factor)
    down = jnp.where(block == 31, 0.0, jnp.maximum(-vx, 0.0) * factor)
    return up[None], down[None]


def first_kernel(*refs):
    pieces, (sine_ref, ty_ref, vy_ref), (v_ref, vx_ref, tx_ref), (field, tables) = refs[:8], refs[8:11], refs[11:14], refs[14:]
    for slot in range(8):
        at = kx_of(slot)
        for x in range(4):
            field[x, :, at, :] = pieces[slot][8 * x : 8 * x + 8]
        vx_ref[at, :] = pieces[slot][32]
    tx_ref[...] = 0.25 * jnp.dot(
        pieces[FIRST][41, 0:8], sine_ref[...], precision=lax.Precision.HIGHEST, preferred_element_type=F32
    )
    for x in range(4):
        tables[x] = left_table(0.5 * tx_ref[x : x + 1, :])
    y_place, half, block = as_host()
    ty = ty_ref[pl.ds(pl.multiple_of(part_index(y_place, half) * 8, 8), 8), :]

    vx = vx_ref[...]
    toward = vx > 0
    rate = jnp.abs(vx) * 0.0625
    vy = jnp.broadcast_to(vy_ref[...], (K, K))
    toward_y = vy > 0
    rate_y = jnp.abs(vy) * 0.125
    zero = jnp.zeros((K, K), F32)
    for pair in range(4):
        right = [right_table(ty[pair * 2 + i : pair * 2 + i + 1, :]) for i in range(2)]
        for x in range(4):
            mine = [field[x, pair * 2 + i] for i in range(2)]
            wigner = times_left(tables[x], mine[0], mine[1])
            for i in range(2):
                y = pair * 2 + i
                total = mine[i] + wigner[i]
                total += inner_drift(mine[i], x, lambda at: field[at, y], toward, rate)
                total += times_right(mine[i], right[i])
                near = [field[x, at] if 0 <= at < 8 else zero for at in (y - 2, y - 1, y + 1, y + 2)]
                one = jnp.where(toward_y, near[1], near[2])
                two = jnp.where(toward_y, near[0], near[3])
                v_ref[x, y] = total - rate_y * slope(mine[i], one, two)


def first_edge_kernel(
    inner_ref, low_a_ref, low_b_ref, high_a_ref, high_b_ref, under_a_ref, under_b_ref, over_a_ref, over_b_ref,
    ring_ref, own_0_ref, own_1_ref, vx_ref, vy_ref, v_ref, *outs,
):
    y_place, half, block = as_host()
    middle = jnp.where(y_place == 3, 1.0, 0.0)
    under_middle, over_middle = y_place == 3 * half, y_place == 3 - 3 * half
    vy = vy_ref[...].reshape(1, 1, K)
    up_y = jnp.maximum(vy, 0.0) * 0.125
    down_y = jnp.maximum(-vy, 0.0) * 0.125
    by_group = ((low_a_ref, high_a_ref, under_a_ref, over_a_ref), (low_b_ref, high_b_ref, under_b_ref, over_b_ref))

    def beside(side, pair, rows):
        slot = SLOTS.index(pair)
        group = int(slot in GROUPS[1])
        return by_group[group][side][slot - GROUPS[group].start, rows]

    for slot in range(8):
        dy, ds = SLOTS[slot]
        at = kx_of(slot)
        group = int(slot in GROUPS[1])
        low_ref, high_ref = by_group[group][:2]
        up, down = rates(vx_ref, at, 0.0625)
        i = slot - GROUPS[group].start
        for x in range(4):
            rows = slice(2 * x, 2 * x + 2)
            if dy == 0:
                across = (own_0_ref, own_1_ref)[ds][33 + 2 * x : 35 + 2 * x]
            elif dy == 2:
                across = ring_ref[ds, rows]
            else:
                across = jnp.where(half == dy // 3, under_b_ref[6 + ds, rows], over_b_ref[6 + ds, rows])
            before, after = ((dy + 3) % 4, ds), ((dy + 1) % 4, ds)
            under = jnp.where(half == 0, beside(2, before, rows), beside(2, after, rows))
            over = jnp.where(half == 0, beside(3, after, rows), beside(3, before, rows))
            under = jnp.where(under_middle, across * middle, under)
            over = jnp.where(over_middle, across * middle, over)
            value = inner_ref[x, :, at, :] + outer_drift(
                x,
                lambda n: low_ref[i, 8 - 8 * n : 16 - 8 * n],
                lambda n: high_ref[i, 8 * n : 8 * n + 8],
                up,
                down,
            )
            bottom = jnp.concatenate([up_y * (4.0 * under[1:2] - under[0:1]), -up_y * under[1:2]], 0)
            top = jnp.concatenate([-down_y * over[0:1], down_y * (4.0 * over[0:1] - over[1:2])], 0)
            value = jnp.concatenate([value[0:2] + bottom, value[2:6], value[6:8] + top], 0)
            v_ref[x, :, at, :] = value
            side = outs[2 * (slot // 4) + x // 2]
            side[slot % 4, 8 * (x % 2) : 8 * (x % 2) + 8] = value


def second_kernel(v_ref, tx_ref, vx_ref, out_ref, tables):
    for x in range(4):
        tables[x] = left_table(tx_ref[x : x + 1, :])

    @pl.loop(0, 4)
    def _(pair):
        vx = vx_ref[...]
        toward = vx > 0
        rate = jnp.abs(vx) * 0.125
        for x in range(4):
            mine = [v_ref[x, pair * 2 + i] for i in range(2)]
            wigner = times_left(tables[x], mine[0], mine[1])
            for i in range(2):
                y = pair * 2 + i
                out_ref[x, y] = wigner[i] + inner_drift(mine[i], x, lambda at: v_ref[at, y], toward, rate)


def second_edge_kernel(slots, inner_ref, low_ref, high_ref, vx_ref, *pieces):
    for i, slot in enumerate(slots):
        at = kx_of(slot)
        up, down = rates(vx_ref, at, 0.125)
        for x in range(4):
            pieces[i][x] = inner_ref[x, :, at, :] + outer_drift(
                x,
                lambda n: low_ref[i, 8 - 8 * n : 16 - 8 * n],
                lambda n: high_ref[i, 8 * n : 8 * n + 8],
                up,
                down,
            )


def final_kernel(local_ref, *refs):
    pieces, out_ref = refs[:8], refs[8]
    for slot in range(8):
        at = rows_to(slot)
        out_ref[:, at] = local_ref[:, at] + pieces[slot][...]


MIB = 1 << 20


def array(*shape):
    return jax.ShapeDtypeStruct(shape, F32)


def params():
    return pltpu.CompilerParams(vmem_limit_bytes=40 * MIB)


def cost(flops, mib):
    return pl.CostEstimate(flops=flops, bytes_accessed=mib * MIB, transcendentals=0)


def call(kernel, outs, scratch=(), flops=0, mib=4):
    def run(*operands):
        return pl.pallas_call(
            kernel,
            out_shape=outs,
            in_specs=[VMEM] * len(operands),
            out_specs=[VMEM] * len(outs) if isinstance(outs, list) else VMEM,
            scratch_shapes=list(scratch),
            compiler_params=params(),
            cost_estimate=cost(flops, mib),
            name=(kernel.func if isinstance(kernel, functools.partial) else kernel).__name__,
        )(*operands)

    return run


def sine_table(sign):
    index = np.arange(K)
    angle = (sign * index[:, None] * index[None, :] % K) * (2.0 * math.pi / K)
    return (np.sin(angle) / K).astype(np.float32)


def back(pairs):
    return [(there, here) for here, there in pairs]


def per_device(density, potential_x, potential_y, speeds_x, speeds_y, upwind_x, upwind_y):
    vel_x = (2 * upwind_x - 1).astype(F32) * speeds_x
    vel_x = jnp.broadcast_to(vel_x[:, None], (16, K))
    vy = ((2 * upwind_y - 1).astype(F32) * speeds_y).reshape(1, K)

    sizes = [33 + 8 * (dy == 0) + (slot == FIRST) for slot, (dy, ds) in enumerate(SLOTS)]
    pieces = call(pack_kernel, [array(size, 16, K) for size in sizes])(density, vel_x, potential_x)
    pieces = [send(piece, exchange_pairs(slot)) for slot, piece in enumerate(pieces)]

    highest = lax.Precision.HIGHEST
    ty = 0.25 * jnp.dot(potential_y, jnp.asarray(sine_table(1)), precision=highest)
    local = call(
        local_kernel, array(4, 64, 16, K), [pltpu.VMEM((2, 4, 68, 16, K), F32)], 4 * 10**9
    )(density, ty, vy)

    low, high, under, over = [None] * 2, [None] * 2, [None] * 2, [None] * 2
    for group in (1, 0):
        slots = GROUPS[group]
        middle = FIRST in slots
        rows = array(len(slots) + 2 * middle, 8, 16, K)
        head, tail, y_low, y_high, *ring = call(
            functools.partial(cut_kernel, slots),
            [array(len(slots), 16, 16, K)] * 2 + [rows] * 2 + [array(2, 8, 16, K)] * middle,
            mib=2,
        )(*pieces[slots.start : slots.stop])
        low[group] = send(tail, x_pairs(1))
        high[group] = send(head, x_pairs(-1))
        under[group] = send(y_high, y_pairs(1))
        over[group] = send(y_low, y_pairs(-1))
        if middle:
            across = send(ring[0], y_pairs(2))
            pieces[0], low[1], high[1], under[1], over[1], across = lax.optimization_barrier(
                (pieces[0], low[1], high[1], under[1], over[1], across)
            )
    left_tables = pltpu.VMEM((4, 2 * K, 2 * K), BF16)
    inner, vx, tx = call(
        first_kernel,
        [array(4, 8, K, K), array(K, K), array(8, K)],
        [pltpu.VMEM((4, 8, K, K), F32), left_tables],
        3 * 10**9,
    )(*pieces, jnp.asarray(sine_table(-1)), ty, vy)
    v, *sides = call(first_edge_kernel, [array(4, 8, K, K)] + [array(4, 16, 16, K)] * 4)(
        inner, *low, *high, *under, *over, across, pieces[FIRST], pieces[FIRST + 1], vx, vy
    )
    low = [send(sides[2 * group + 1], x_pairs(1)) for group in range(2)]
    high = [send(sides[2 * group], x_pairs(-1)) for group in range(2)]
    inner = call(second_kernel, array(4, 8, K, K), [left_tables], 2 * 10**9)(v, tx, vx)
    pieces = []
    for group, slots in enumerate((range(0, 4), range(4, 8))):
        cut = call(functools.partial(second_edge_kernel, slots), [array(4, 8, 16, K)] * 4, mib=2)(
            inner, low[group], high[group], vx
        )
        pieces += [send(piece, back(exchange_pairs(slot))) for slot, piece in zip(slots, cut)]

    def by_x(*shape):
        return pl.BlockSpec((1, *shape), lambda x: (x, 0, 0, 0))

    return pl.pallas_call(
        final_kernel,
        grid=(4,),
        out_shape=array(4, 64, 16, K),
        in_specs=[by_x(64, 16, K)] + [by_x(8, 16, K)] * 8,
        out_specs=by_x(64, 16, K),
        compiler_params=params(),
        cost_estimate=cost(0, 6),
        name="final_kernel",
    )(local, *pieces)


def solution(mesh):
    in_specs = (P("gx", None, "ka", None), P("gx", None), P(), P("ka"), P(), P("ka"), P())
    out_specs = P("gx", None, "ka", None)
    return jax.shard_map(
        per_device, mesh=mesh, in_specs=in_specs, out_specs=out_specs, check_vma=False
    )
```

```python
import functools
import math

import jax
import jax.numpy as jnp
import numpy as np
from jax import lax
from jax.experimental import pallas as pl
from jax.experimental.pallas import tpu as pltpu
from jax.sharding import PartitionSpec as P


F32 = jnp.float32
BF16 = jnp.bfloat16
K = 128
AXES = ("gx", "ka")
SLOTS = [(2, 0), (2, 1), (1, 0), (1, 1), (3, 0), (3, 1), (0, 0), (0, 1)]
GROUPS = ((2, 3, 4, 5), (0, 1, 6, 7))
FIRST, SECOND = SLOTS.index((0, 0)), SLOTS.index((0, 1))
VMEM = pl.BlockSpec(memory_space=pltpu.VMEM)


def flat(x, y, z, core):
    return ((x * 4 + z % 4) * 2 + core) * 8 + y * 2 + z // 4


def place(block, part):
    x, low, core = block // 8, block // 2 % 4, block % 2
    half = part // 4
    y = part if half == 0 else 7 - part
    z = (low + 2 if x % 2 == 0 else 5 - low) + 4 * half
    return flat(x, y, z % 8, core)


def part_of(y, half):
    return y if half == 0 else 7 - y


def slot_part(ka, slot):
    dy, ds = SLOTS[slot]
    return part_of((ka // 2 + dy) % 4, (ka % 2) ^ ds)


def exchange_pairs(slot):
    return [
        (block * 8 + ka, place(block, slot_part(ka, slot)))
        for block in range(32)
        for ka in range(8)
    ]


def x_pairs(step):
    return [
        (place(block, part), place((block + step) % 32, part))
        for block in range(32)
        for part in range(8)
    ]


def y_pairs(step):
    return [
        (place(block, 4 * half + part), place(block, 4 * half + (part + step) % 4))
        for block in range(32)
        for half in range(2)
        for part in range(4)
    ]


def send(value, pairs):
    return lax.ppermute(value, AXES, pairs)


def as_source():
    ka = lax.axis_index("ka")
    return ka >> 1, ka & 1


def as_host():
    gx, ka = lax.axis_index("gx"), lax.axis_index("ka")
    z = (ka & 1) * 4 + ((gx >> 1) & 3)
    turn = jnp.where(((gx >> 3) & 1) == 0, z - 2, 5 - z) & 7
    return ka >> 1, turn >> 2, (gx & 25) + (turn & 3) * 2


def part_index(y, half):
    return y + half * (7 - 2 * y)


def rows_to(slot):
    y, half = as_source()
    dy, ds = SLOTS[slot]
    return pl.ds(pl.multiple_of(part_index((y + dy) & 3, half ^ ds) * 8, 8), 8)


def kx_of(slot):
    y, half, block = as_host()
    dy, ds = SLOTS[slot]
    return pl.ds(pl.multiple_of((((y - dy) & 3) * 2 + (half ^ ds)) * 16, 16), 16)


def halves(value):
    high = value.astype(BF16)
    return high, (value - high.astype(F32)).astype(BF16)


def circulant(row):
    return pltpu.roll(jnp.broadcast_to(row, (K, K)), 0, 1, stride=1, stride_axis=0)


def right_table(row):
    high, low = halves(circulant(row))
    return jnp.concatenate(
        [
            jnp.concatenate([high, low], 1),
            jnp.concatenate([high, jnp.zeros_like(low)], 1),
        ],
        0,
    )


def left_table(row):
    high, low = halves(circulant(row))
    return jnp.concatenate(
        [
            jnp.concatenate([high, high], 1),
            jnp.concatenate([low, jnp.zeros_like(low)], 1),
        ],
        0,
    )


def times_right(rows, table):
    both = jnp.dot(jnp.concatenate(halves(rows), 1), table, preferred_element_type=F32)
    return both[:, :K] + both[:, K:]


def times_left(table, first, second):
    high_0, low_0 = halves(first)
    high_1, low_1 = halves(second)
    stacked = jnp.concatenate(
        [jnp.concatenate([high_0, high_1], 1), jnp.concatenate([low_0, low_1], 1)], 0
    )
    both = jnp.dot(table, stacked, preferred_element_type=F32)
    both = both[:K] + both[K:]
    return both[:, :K], both[:, K:]


def slope(center, one, two):
    return 3.0 * center - 4.0 * one + two


def local_kernel(g_ref, ty_ref, vy_ref, out_ref, pad):
    vy = vy_ref[...].reshape(1, 1, K)
    toward = jnp.broadcast_to(vy > 0, (4, 16, K))
    rate = jnp.abs(vy) * 0.125

    def step(value, one_low, two_low, one_high, two_high, table):
        one = jnp.where(toward, one_low, one_high)
        two = jnp.where(toward, two_low, two_high)
        wigner = times_right(value.reshape(64, K), table).reshape(4, 16, K)
        return wigner - rate * slope(value, one, two)

    edge = jnp.zeros((4, 2, 16, K), F32)
    pad[0, :, 0:2] = edge
    pad[0, :, 66:68] = edge
    pad[1, :, 0:2] = edge
    pad[1, :, 66:68] = edge
    for y in range(64):
        pad[0, :, y + 2] = g_ref[:, y]

    def turn(source, into):
        @pl.loop(0, 8)
        def _(group):
            block = ty_ref[pl.ds(pl.multiple_of(group * 8, 8), 8), :]
            for inner in range(8):
                y = group * 8 + inner
                value = pad[source, :, y + 2]
                moved = step(
                    value,
                    pad[source, :, y + 1],
                    pad[source, :, y],
                    pad[source, :, y + 3],
                    pad[source, :, y + 4],
                    right_table(block[inner : inner + 1]),
                )
                into(y, value, moved)

    def first(y, value, moved):
        pad[1, :, y + 2] = value + moved

    def second(y, value, moved):
        out_ref[:, y] = 0.5 * (pad[0, :, y + 2] + value + moved)

    turn(0, first)
    turn(1, second)


def pack_kernel(g_ref, vel_ref, potential_ref, *pieces):
    y, half = as_source()
    for slot in range(8):
        at = rows_to(slot)
        for x in range(4):
            pieces[slot][8 * x : 8 * x + 8] = g_ref[x, at]
        pieces[slot][32] = vel_ref[...]
        dy, ds = SLOTS[slot]
        if dy == 0:
            at = pl.ds(32 - 2 * (half ^ ds), 2)
            for x in range(4):
                pieces[slot][33 + 2 * x : 35 + 2 * x] = g_ref[x, at]
    pieces[FIRST][41, 0:4] = potential_ref[...]
    pieces[FIRST][41, 4:16] = jnp.zeros((12, K), F32)


def cut_kernel(*refs):
    pieces, (head_ref, tail_ref, y_low_ref, y_high_ref, across_ref) = refs[:8], refs[8:]
    for i in range(8):
        head_ref[i] = pieces[i][0:16]
        tail_ref[i] = pieces[i][16:32]
        for x in range(4):
            y_low_ref[i, 2 * x : 2 * x + 2] = pieces[i][8 * x : 8 * x + 2]
            y_high_ref[i, 2 * x : 2 * x + 2] = pieces[i][8 * x + 6 : 8 * x + 8]
        dy, ds = SLOTS[i]
        if dy == 0:
            rows = pieces[i][33:41]
            y_low_ref[8 + ds] = rows
            y_high_ref[8 + ds] = rows
            across_ref[ds] = rows


def inner_drift(center, x, layer, toward, rate):
    total = 3.0 * center
    for step, factor in ((1, -4.0), (2, 1.0)):
        low = layer(x - step) if x - step >= 0 else None
        high = layer(x + step) if x + step <= 3 else None
        if low is None:
            if high is not None:
                total += factor * jnp.where(toward, 0.0, high)
        elif high is None:
            total += factor * jnp.where(toward, low, 0.0)
        else:
            total += factor * jnp.where(toward, low, high)
    return -rate * total


def outer_drift(x, low, high, up, down):
    if x == 0:
        return up * (4.0 * low(0) - low(1))
    if x == 1:
        return -up * low(0)
    if x == 2:
        return -down * high(0)
    return down * (4.0 * high(0) - high(1))


def rates(vx_ref, at, factor):
    vx = vx_ref[at, :]
    block = as_host()[2]
    up = jnp.where(block == 0, 0.0, jnp.maximum(vx, 0.0) * factor)
    down = jnp.where(block == 31, 0.0, jnp.maximum(-vx, 0.0) * factor)
    return up[None], down[None]


def first_kernel(*refs):
    pieces, (sine_ref, ty_ref, vy_ref), (v_ref, vx_ref, tx_ref), (field, tables) = refs[:8], refs[8:11], refs[11:14], refs[14:]
    for slot in range(8):
        at = kx_of(slot)
        for x in range(4):
            field[x, :, at, :] = pieces[slot][8 * x : 8 * x + 8]
        vx_ref[at, :] = pieces[slot][32]
    tx_ref[...] = 0.25 * jnp.dot(
        pieces[FIRST][41, 0:8], sine_ref[...], precision=lax.Precision.HIGHEST, preferred_element_type=F32
    )
    for x in range(4):
        tables[x] = left_table(0.5 * tx_ref[x : x + 1, :])
    y_place, half, block = as_host()
    ty = ty_ref[pl.ds(pl.multiple_of(part_index(y_place, half) * 8, 8), 8), :]

    vx = vx_ref[...]
    toward = vx > 0
    rate = jnp.abs(vx) * 0.0625
    vy = jnp.broadcast_to(vy_ref[...], (K, K))
    toward_y = vy > 0
    rate_y = jnp.abs(vy) * 0.125
    zero = jnp.zeros((K, K), F32)
    for pair in range(4):
        right = [right_table(ty[pair * 2 + i : pair * 2 + i + 1, :]) for i in range(2)]
        for x in range(4):
            mine = [field[x, pair * 2 + i] for i in range(2)]
            wigner = times_left(tables[x], mine[0], mine[1])
            for i in range(2):
                y = pair * 2 + i
                total = mine[i] + wigner[i]
                total += inner_drift(mine[i], x, lambda at: field[at, y], toward, rate)
                total += times_right(mine[i], right[i])
                near = [field[x, at] if 0 <= at < 8 else zero for at in (y - 2, y - 1, y + 1, y + 2)]
                one = jnp.where(toward_y, near[1], near[2])
                two = jnp.where(toward_y, near[0], near[3])
                v_ref[x, y] = total - rate_y * slope(mine[i], one, two)


def first_edge_kernel(
    inner_ref, low_ref, high_ref, under_ref, over_ref, ring_ref, own_0_ref, own_1_ref, vx_ref, vy_ref, v_ref, *outs
):
    y_place, half, block = as_host()
    middle = jnp.where(y_place == 3, 1.0, 0.0)
    under_middle, over_middle = y_place == 3 * half, y_place == 3 - 3 * half
    vy = vy_ref[...].reshape(1, 1, K)
    up_y = jnp.maximum(vy, 0.0) * 0.125
    down_y = jnp.maximum(-vy, 0.0) * 0.125

    def beside(ref, pair, rows):
        return ref[SLOTS.index(pair), rows]

    for slot in range(8):
        dy, ds = SLOTS[slot]
        at = kx_of(slot)
        up, down = rates(vx_ref, at, 0.0625)
        for x in range(4):
            rows = slice(2 * x, 2 * x + 2)
            if dy == 0:
                across = (own_0_ref, own_1_ref)[ds][33 + 2 * x : 35 + 2 * x]
            elif dy == 2:
                across = ring_ref[ds, rows]
            else:
                across = jnp.where(half == dy // 3, under_ref[8 + ds, rows], over_ref[8 + ds, rows])
            before, after = ((dy + 3) % 4, ds), ((dy + 1) % 4, ds)
            under = jnp.where(half == 0, beside(under_ref, before, rows), beside(under_ref, after, rows))
            over = jnp.where(half == 0, beside(over_ref, after, rows), beside(over_ref, before, rows))
            under = jnp.where(under_middle, across * middle, under)
            over = jnp.where(over_middle, across * middle, over)
            value = inner_ref[x, :, at, :] + outer_drift(
                x,
                lambda n: low_ref[slot, 8 - 8 * n : 16 - 8 * n],
                lambda n: high_ref[slot, 8 * n : 8 * n + 8],
                up,
                down,
            )
            bottom = jnp.concatenate([up_y * (4.0 * under[1:2] - under[0:1]), -up_y * under[1:2]], 0)
            top = jnp.concatenate([-down_y * over[0:1], down_y * (4.0 * over[0:1] - over[1:2])], 0)
            value = jnp.concatenate([value[0:2] + bottom, value[2:6], value[6:8] + top], 0)
            v_ref[x, :, at, :] = value
            group = int(slot in GROUPS[1])
            side = outs[2 * group + x // 2]
            side[GROUPS[group].index(slot), 8 * (x % 2) : 8 * (x % 2) + 8] = value


def second_kernel(v_ref, tx_ref, vx_ref, out_ref, tables):
    for x in range(4):
        tables[x] = left_table(tx_ref[x : x + 1, :])

    @pl.loop(0, 4)
    def _(pair):
        vx = vx_ref[...]
        toward = vx > 0
        rate = jnp.abs(vx) * 0.125
        for x in range(4):
            mine = [v_ref[x, pair * 2 + i] for i in range(2)]
            wigner = times_left(tables[x], mine[0], mine[1])
            for i in range(2):
                y = pair * 2 + i
                out_ref[x, y] = wigner[i] + inner_drift(mine[i], x, lambda at: v_ref[at, y], toward, rate)


def second_edge_kernel(slots, inner_ref, low_ref, high_ref, vx_ref, *pieces):
    for i, slot in enumerate(slots):
        at = kx_of(slot)
        up, down = rates(vx_ref, at, 0.125)
        for x in range(4):
            pieces[i][x] = inner_ref[x, :, at, :] + outer_drift(
                x,
                lambda n: low_ref[i, 8 - 8 * n : 16 - 8 * n],
                lambda n: high_ref[i, 8 * n : 8 * n + 8],
                up,
                down,
            )


def final_kernel(local_ref, *refs):
    pieces, out_ref = refs[:8], refs[8]
    for slot in range(8):
        at = rows_to(slot)
        out_ref[:, at] = local_ref[:, at] + pieces[slot][...]


MIB = 1 << 20


def array(*shape):
    return jax.ShapeDtypeStruct(shape, F32)


def params():
    return pltpu.CompilerParams(vmem_limit_bytes=40 * MIB)


def cost(flops, mib):
    return pl.CostEstimate(flops=flops, bytes_accessed=mib * MIB, transcendentals=0)


def call(kernel, outs, scratch=(), flops=0, mib=4):
    def run(*operands):
        return pl.pallas_call(
            kernel,
            out_shape=outs,
            in_specs=[VMEM] * len(operands),
            out_specs=[VMEM] * len(outs) if isinstance(outs, list) else VMEM,
            scratch_shapes=list(scratch),
            compiler_params=params(),
            cost_estimate=cost(flops, mib),
            name=(kernel.func if isinstance(kernel, functools.partial) else kernel).__name__,
        )(*operands)

    return run


def sine_table(sign):
    index = np.arange(K)
    angle = (sign * index[:, None] * index[None, :] % K) * (2.0 * math.pi / K)
    return (np.sin(angle) / K).astype(np.float32)


def back(pairs):
    return [(there, here) for here, there in pairs]


def per_device(density, potential_x, potential_y, speeds_x, speeds_y, upwind_x, upwind_y):
    vel_x = (2 * upwind_x - 1).astype(F32) * speeds_x
    vel_x = jnp.broadcast_to(vel_x[:, None], (16, K))
    vy = ((2 * upwind_y - 1).astype(F32) * speeds_y).reshape(1, K)

    sizes = [33 + 8 * (dy == 0) + (slot == FIRST) for slot, (dy, ds) in enumerate(SLOTS)]
    pieces = call(pack_kernel, [array(size, 16, K) for size in sizes])(density, vel_x, potential_x)
    pieces = [send(piece, exchange_pairs(slot)) for slot, piece in enumerate(pieces)]

    highest = lax.Precision.HIGHEST
    ty = 0.25 * jnp.dot(potential_y, jnp.asarray(sine_table(1)), precision=highest)
    local = call(
        local_kernel, array(4, 64, 16, K), [pltpu.VMEM((2, 4, 68, 16, K), F32)], 4 * 10**9
    )(density, ty, vy)

    head, tail, y_low, y_high, across = call(
        cut_kernel, [array(8, 16, 16, K)] * 2 + [array(10, 8, 16, K)] * 2 + [array(2, 8, 16, K)]
    )(*pieces)
    under, over = send(y_high, y_pairs(1)), send(y_low, y_pairs(-1))
    low, high = send(tail, x_pairs(1)), send(head, x_pairs(-1))
    across = send(across, y_pairs(2))
    left_tables = pltpu.VMEM((4, 2 * K, 2 * K), BF16)
    inner, vx, tx = call(
        first_kernel,
        [array(4, 8, K, K), array(K, K), array(8, K)],
        [pltpu.VMEM((4, 8, K, K), F32), left_tables],
        3 * 10**9,
    )(*pieces, jnp.asarray(sine_table(-1)), ty, vy)
    v, *sides = call(first_edge_kernel, [array(4, 8, K, K)] + [array(4, 16, 16, K)] * 4)(
        inner, low, high, under, over, across, pieces[FIRST], pieces[SECOND], vx, vy
    )
    low = [send(sides[2 * group + 1], x_pairs(1)) for group in range(2)]
    high = [send(sides[2 * group], x_pairs(-1)) for group in range(2)]
    inner = call(second_kernel, array(4, 8, K, K), [left_tables], 2 * 10**9)(v, tx, vx)
    pieces = [None] * 8
    for group, slots in enumerate(GROUPS):
        cut = call(functools.partial(second_edge_kernel, slots), [array(4, 8, 16, K)] * 4, mib=2)(
            inner, low[group], high[group], vx
        )
        for slot, piece in zip(slots, cut):
            pieces[slot] = send(piece, back(exchange_pairs(slot)))

    def by_x(*shape):
        return pl.BlockSpec((1, *shape), lambda x: (x, 0, 0, 0))

    return pl.pallas_call(
        final_kernel,
        grid=(4,),
        out_shape=array(4, 64, 16, K),
        in_specs=[by_x(64, 16, K)] + [by_x(8, 16, K)] * 8,
        out_specs=by_x(64, 16, K),
        compiler_params=params(),
        cost_estimate=cost(0, 6),
        name="final_kernel",
    )(local, *pieces)


def solution(mesh):
    in_specs = (P("gx", None, "ka", None), P("gx", None), P(), P("ka"), P(), P("ka"), P())
    out_specs = P("gx", None, "ka", None)
    return jax.shard_map(
        per_device, mesh=mesh, in_specs=in_specs, out_specs=out_specs, check_vma=False
    )
```

```python
import functools
import math

import jax
import jax.numpy as jnp
import numpy as np
from jax import lax
from jax.experimental import pallas as pl
from jax.experimental.pallas import tpu as pltpu
from jax.sharding import PartitionSpec as P


F32 = jnp.float32
BF16 = jnp.bfloat16
K = 128
AXES = ("gx", "ka")
SLOTS = [(2, 0), (2, 1), (1, 0), (1, 1), (3, 0), (3, 1), (0, 0), (0, 1)]
GROUPS = ((2, 3, 4, 5), (0, 1, 6, 7))
FIRST, SECOND = SLOTS.index((0, 0)), SLOTS.index((0, 1))
VMEM = pl.BlockSpec(memory_space=pltpu.VMEM)


def flat(x, y, z, core):
    return ((x * 4 + z % 4) * 2 + core) * 8 + y * 2 + z // 4


def place(block, part):
    x, low, core = block // 8, block // 2 % 4, block % 2
    half = part // 4
    y = part if half == 0 else 7 - part
    return flat(x, y, (low + 2 + 4 * (half ^ x % 2)) % 8, core)


def part_of(y, half):
    return y if half == 0 else 7 - y


def slot_part(ka, slot):
    dy, ds = SLOTS[slot]
    return part_of((ka // 2 + dy) % 4, (ka % 2) ^ ds)


def exchange_pairs(slot):
    return [
        (block * 8 + ka, place(block, slot_part(ka, slot)))
        for block in range(32)
        for ka in range(8)
    ]


def x_pairs(step):
    return [
        (place(block, part), place((block + step) % 32, part))
        for block in range(32)
        for part in range(8)
    ]


def y_pairs(step):
    return [
        (place(block, 4 * half + part), place(block, 4 * half + (part + step) % 4))
        for block in range(32)
        for half in range(2)
        for part in range(4)
    ]


def middle_pairs(y):
    return [
        (place(block, part_of(y, half)), place(block, part_of(3, half)))
        for block in range(32)
        for half in range(2)
    ]


def send(value, pairs):
    return lax.ppermute(value, AXES, pairs)


def as_source():
    ka = lax.axis_index("ka")
    return ka >> 1, ka & 1


def as_host():
    gx, ka = lax.axis_index("gx"), lax.axis_index("ka")
    z = (ka & 1) * 4 + ((gx >> 1) & 3)
    turn = (z - 2) & 7
    return ka >> 1, (turn >> 2) ^ ((gx >> 3) & 1), (gx & 25) + (turn & 3) * 2


def part_index(y, half):
    return y + half * (7 - 2 * y)


def rows_to(slot):
    y, half = as_source()
    dy, ds = SLOTS[slot]
    return pl.ds(pl.multiple_of(part_index((y + dy) & 3, half ^ ds) * 8, 8), 8)


def kx_of(slot):
    y, half, block = as_host()
    dy, ds = SLOTS[slot]
    return pl.ds(pl.multiple_of((((y - dy) & 3) * 2 + (half ^ ds)) * 16, 16), 16)


def halves(value):
    high = value.astype(BF16)
    return high, (value - high.astype(F32)).astype(BF16)


def circulant(row):
    return pltpu.roll(jnp.broadcast_to(row, (K, K)), 0, 1, stride=1, stride_axis=0)


def right_table(row):
    high, low = halves(circulant(row))
    return jnp.concatenate(
        [
            jnp.concatenate([high, low], 1),
            jnp.concatenate([high, jnp.zeros_like(low)], 1),
        ],
        0,
    )


def left_table(row):
    high, low = halves(circulant(row))
    return jnp.concatenate(
        [
            jnp.concatenate([high, high], 1),
            jnp.concatenate([low, jnp.zeros_like(low)], 1),
        ],
        0,
    )


def times_right(rows, table):
    both = jnp.dot(jnp.concatenate(halves(rows), 1), table, preferred_element_type=F32)
    return both[:, :K] + both[:, K:]


def times_left(table, first, second):
    high_0, low_0 = halves(first)
    high_1, low_1 = halves(second)
    stacked = jnp.concatenate(
        [jnp.concatenate([high_0, high_1], 1), jnp.concatenate([low_0, low_1], 1)], 0
    )
    both = jnp.dot(table, stacked, preferred_element_type=F32)
    both = both[:K] + both[K:]
    return both[:, :K], both[:, K:]


def slope(center, one, two):
    return 3.0 * center - 4.0 * one + two


def local_kernel(g_ref, ty_ref, vy_ref, out_ref, pad):
    vy = vy_ref[...].reshape(1, 1, K)
    toward = jnp.broadcast_to(vy > 0, (4, 16, K))
    rate = jnp.abs(vy) * 0.125

    def step(value, one_low, two_low, one_high, two_high, table):
        one = jnp.where(toward, one_low, one_high)
        two = jnp.where(toward, two_low, two_high)
        wigner = times_right(value.reshape(64, K), table).reshape(4, 16, K)
        return wigner - rate * slope(value, one, two)

    edge = jnp.zeros((4, 2, 16, K), F32)
    pad[0, :, 0:2] = edge
    pad[0, :, 66:68] = edge
    pad[1, :, 0:2] = edge
    pad[1, :, 66:68] = edge
    for y in range(64):
        pad[0, :, y + 2] = g_ref[:, y]

    def turn(source, into):
        @pl.loop(0, 8)
        def _(group):
            block = ty_ref[pl.ds(pl.multiple_of(group * 8, 8), 8), :]
            for inner in range(8):
                y = group * 8 + inner
                value = pad[source, :, y + 2]
                moved = step(
                    value,
                    pad[source, :, y + 1],
                    pad[source, :, y],
                    pad[source, :, y + 3],
                    pad[source, :, y + 4],
                    right_table(block[inner : inner + 1]),
                )
                into(y, value, moved)

    def first(y, value, moved):
        pad[1, :, y + 2] = value + moved

    def second(y, value, moved):
        out_ref[:, y] = 0.5 * (pad[0, :, y + 2] + value + moved)

    turn(0, first)
    turn(1, second)


def pack_kernel(g_ref, vel_ref, potential_ref, *pieces):
    y, half = as_source()
    for slot in range(8):
        at = rows_to(slot)
        for x in range(4):
            pieces[slot][8 * x : 8 * x + 8] = g_ref[x, at]
        pieces[slot][32] = vel_ref[...]
        dy, ds = SLOTS[slot]
        if dy == 0:
            at = pl.ds(32 - 2 * (half ^ ds), 2)
            for x in range(4):
                pieces[slot][33 + 2 * x : 35 + 2 * x] = g_ref[x, at]
    pieces[FIRST][41, 0:4] = potential_ref[...]
    pieces[FIRST][41, 4:16] = jnp.zeros((12, K), F32)


def across_kernel(first_ref, second_ref, out_ref):
    out_ref[0] = first_ref[33:41]
    out_ref[1] = second_ref[33:41]


def cut_kernel(*refs):
    pieces, (head_ref, tail_ref) = refs[:4], refs[4:]
    for i in range(4):
        head_ref[i] = pieces[i][0:16]
        tail_ref[i] = pieces[i][16:32]


def rows_kernel(*refs):
    pieces, (bottom_ref, top_ref) = refs[:8], refs[8:]
    for slot in range(8):
        for x in range(4):
            bottom_ref[slot, 2 * x : 2 * x + 2] = pieces[slot][8 * x : 8 * x + 2]
            top_ref[slot, 2 * x : 2 * x + 2] = pieces[slot][8 * x + 6 : 8 * x + 8]


def inner_drift(center, x, layer, toward, rate):
    total = 3.0 * center
    for step, factor in ((1, -4.0), (2, 1.0)):
        low = layer(x - step) if x - step >= 0 else None
        high = layer(x + step) if x + step <= 3 else None
        if low is None:
            if high is not None:
                total += factor * jnp.where(toward, 0.0, high)
        elif high is None:
            total += factor * jnp.where(toward, low, 0.0)
        else:
            total += factor * jnp.where(toward, low, high)
    return -rate * total


def outer_drift(x, low, high, up, down):
    if x == 0:
        return up * (4.0 * low(0) - low(1))
    if x == 1:
        return -up * low(0)
    if x == 2:
        return -down * high(0)
    return down * (4.0 * high(0) - high(1))


def rates(vx_ref, at, factor):
    vx = vx_ref[at, :]
    block = as_host()[2]
    up = jnp.where(block == 0, 0.0, jnp.maximum(vx, 0.0) * factor)
    down = jnp.where(block == 31, 0.0, jnp.maximum(-vx, 0.0) * factor)
    return up[None], down[None]


def first_kernel(*refs):
    pieces, (sine_ref, ty_ref, vy_ref), (v_ref, vx_ref, tx_ref), (field, tables) = refs[:8], refs[8:11], refs[11:14], refs[14:]
    for slot in range(8):
        at = kx_of(slot)
        for x in range(4):
            field[x, :, at, :] = pieces[slot][8 * x : 8 * x + 8]
        vx_ref[at, :] = pieces[slot][32]
    tx_ref[...] = 0.25 * jnp.dot(
        pieces[FIRST][41, 0:8], sine_ref[...], precision=lax.Precision.HIGHEST, preferred_element_type=F32
    )
    for x in range(4):
        tables[x] = left_table(0.5 * tx_ref[x : x + 1, :])
    y_place, half, block = as_host()
    ty = ty_ref[pl.ds(pl.multiple_of(part_index(y_place, half) * 8, 8), 8), :]

    vx = vx_ref[...]
    toward = vx > 0
    rate = jnp.abs(vx) * 0.0625
    vy = jnp.broadcast_to(vy_ref[...], (K, K))
    toward_y = vy > 0
    rate_y = jnp.abs(vy) * 0.125
    zero = jnp.zeros((K, K), F32)
    for pair in range(4):
        right = [right_table(ty[pair * 2 + i : pair * 2 + i + 1, :]) for i in range(2)]
        for x in range(4):
            mine = [field[x, pair * 2 + i] for i in range(2)]
            wigner = times_left(tables[x], mine[0], mine[1])
            for i in range(2):
                y = pair * 2 + i
                total = mine[i] + wigner[i]
                total += inner_drift(mine[i], x, lambda at: field[at, y], toward, rate)
                total += times_right(mine[i], right[i])
                near = [field[x, at] if 0 <= at < 8 else zero for at in (y - 2, y - 1, y + 1, y + 2)]
                one = jnp.where(toward_y, near[1], near[2])
                two = jnp.where(toward_y, near[0], near[3])
                v_ref[x, y] = total - rate_y * slope(mine[i], one, two)


def first_edge_kernel(
    inner_ref, low_a_ref, low_b_ref, high_a_ref, high_b_ref, under_ref, over_ref, from_0_ref, from_1_ref, from_2_ref, own_0_ref, own_1_ref, vx_ref, vy_ref, v_ref, *outs
):
    y_place, half, block = as_host()
    middle = jnp.where(y_place == 3, 1.0, 0.0)
    under_middle, over_middle = y_place == 3 * half, y_place == 3 - 3 * half
    vy = vy_ref[...].reshape(1, 1, K)
    up_y = jnp.maximum(vy, 0.0) * 0.125
    down_y = jnp.maximum(-vy, 0.0) * 0.125

    def beside(ref, pair, rows):
        return ref[SLOTS.index(pair), rows]

    for slot in range(8):
        dy, ds = SLOTS[slot]
        at = kx_of(slot)
        up, down = rates(vx_ref, at, 0.0625)
        group = int(slot in GROUPS[1])
        i = GROUPS[group].index(slot)
        low_ref, high_ref = ((low_a_ref, high_a_ref), (low_b_ref, high_b_ref))[group]
        for x in range(4):
            rows = slice(2 * x, 2 * x + 2)
            if dy == 0:
                across = (own_0_ref, own_1_ref)[ds][33 + 2 * x : 35 + 2 * x]
            else:
                across = (from_2_ref, from_1_ref, from_0_ref)[dy - 1][ds, rows]
            before, after = ((dy + 3) % 4, ds), ((dy + 1) % 4, ds)
            under = jnp.where(half == 0, beside(under_ref, before, rows), beside(under_ref, after, rows))
            over = jnp.where(half == 0, beside(over_ref, after, rows), beside(over_ref, before, rows))
            under = jnp.where(under_middle, across * middle, under)
            over = jnp.where(over_middle, across * middle, over)
            value = inner_ref[x, :, at, :] + outer_drift(
                x,
                lambda n: low_ref[i, 8 - 8 * n : 16 - 8 * n],
                lambda n: high_ref[i, 8 * n : 8 * n + 8],
                up,
                down,
            )
            bottom = jnp.concatenate([up_y * (4.0 * under[1:2] - under[0:1]), -up_y * under[1:2]], 0)
            top = jnp.concatenate([-down_y * over[0:1], down_y * (4.0 * over[0:1] - over[1:2])], 0)
            value = jnp.concatenate([value[0:2] + bottom, value[2:6], value[6:8] + top], 0)
            v_ref[x, :, at, :] = value
            side = outs[2 * group + x // 2]
            side[i, 8 * (x % 2) : 8 * (x % 2) + 8] = value


def second_kernel(v_ref, tx_ref, vx_ref, out_ref, tables):
    for x in range(4):
        tables[x] = left_table(tx_ref[x : x + 1, :])

    @pl.loop(0, 4)
    def _(pair):
        vx = vx_ref[...]
        toward = vx > 0
        rate = jnp.abs(vx) * 0.125
        for x in range(4):
            mine = [v_ref[x, pair * 2 + i] for i in range(2)]
            wigner = times_left(tables[x], mine[0], mine[1])
            for i in range(2):
                y = pair * 2 + i
                out_ref[x, y] = wigner[i] + inner_drift(mine[i], x, lambda at: v_ref[at, y], toward, rate)


def second_edge_kernel(slots, inner_ref, low_ref, high_ref, vx_ref, *pieces):
    for i, slot in enumerate(slots):
        at = kx_of(slot)
        up, down = rates(vx_ref, at, 0.125)
        for x in range(4):
            pieces[i][x] = inner_ref[x, :, at, :] + outer_drift(
                x,
                lambda n: low_ref[i, 8 - 8 * n : 16 - 8 * n],
                lambda n: high_ref[i, 8 * n : 8 * n + 8],
                up,
                down,
            )


def final_kernel(local_ref, *refs):
    pieces, out_ref = refs[:8], refs[8]
    for slot in range(8):
        at = rows_to(slot)
        out_ref[:, at] = local_ref[:, at] + pieces[slot][...]


MIB = 1 << 20


def array(*shape):
    return jax.ShapeDtypeStruct(shape, F32)


def params():
    return pltpu.CompilerParams(vmem_limit_bytes=40 * MIB)


def cost(flops, mib):
    return pl.CostEstimate(flops=flops, bytes_accessed=mib * MIB, transcendentals=0)


def call(kernel, outs, scratch=(), flops=0, mib=4):
    def run(*operands):
        return pl.pallas_call(
            kernel,
            out_shape=outs,
            in_specs=[VMEM] * len(operands),
            out_specs=[VMEM] * len(outs) if isinstance(outs, list) else VMEM,
            scratch_shapes=list(scratch),
            compiler_params=params(),
            cost_estimate=cost(flops, mib),
            name=(kernel.func if isinstance(kernel, functools.partial) else kernel).__name__,
        )(*operands)

    return run


def sine_table(sign):
    index = np.arange(K)
    angle = (sign * index[:, None] * index[None, :] % K) * (2.0 * math.pi / K)
    return (np.sin(angle) / K).astype(np.float32)


def back(pairs):
    return [(there, here) for here, there in pairs]


def per_device(density, potential_x, potential_y, speeds_x, speeds_y, upwind_x, upwind_y):
    vel_x = (2 * upwind_x - 1).astype(F32) * speeds_x
    vel_x = jnp.broadcast_to(vel_x[:, None], (16, K))
    vy = ((2 * upwind_y - 1).astype(F32) * speeds_y).reshape(1, K)

    sizes = [33 + 8 * (dy == 0) + (slot == FIRST) for slot, (dy, ds) in enumerate(SLOTS)]
    pieces = call(pack_kernel, [array(size, 16, K) for size in sizes])(density, vel_x, potential_x)
    pieces = [send(piece, exchange_pairs(slot)) for slot, piece in enumerate(pieces)]

    highest = lax.Precision.HIGHEST
    ty = 0.25 * jnp.dot(potential_y, jnp.asarray(sine_table(1)), precision=highest)
    local = call(
        local_kernel, array(4, 64, 16, K), [pltpu.VMEM((2, 4, 68, 16, K), F32)], 4 * 10**9
    )(density, ty, vy)

    across = call(across_kernel, array(2, 8, 16, K), mib=0)(pieces[FIRST], pieces[SECOND])
    across = [send(across, middle_pairs(y)) for y in range(3)]
    low, high = [None] * 2, [None] * 2
    for group in (1, 0):
        mine = [pieces[slot] for slot in GROUPS[group]]
        if group == 0:
            *mine, low[1], high[1], across[0], across[1], across[2] = lax.optimization_barrier((*mine, low[1], high[1], *across))
        head, tail = call(cut_kernel, [array(4, 16, 16, K)] * 2, mib=2)(*mine)
        low[group] = send(tail, x_pairs(1))
        high[group] = send(head, x_pairs(-1))
    y_low, y_high = call(rows_kernel, [array(8, 8, 16, K)] * 2, mib=2)(*pieces)
    under, over = send(y_high, y_pairs(1)), send(y_low, y_pairs(-1))
    left_tables = pltpu.VMEM((4, 2 * K, 2 * K), BF16)
    inner, vx, tx = call(
        first_kernel,
        [array(4, 8, K, K), array(K, K), array(8, K)],
        [pltpu.VMEM((4, 8, K, K), F32), left_tables],
        3 * 10**9,
    )(*pieces, jnp.asarray(sine_table(-1)), ty, vy)
    v, *sides = call(first_edge_kernel, [array(4, 8, K, K)] + [array(4, 16, 16, K)] * 4)(
        inner, *low, *high, under, over, *across, pieces[FIRST], pieces[SECOND], vx, vy
    )
    low = [send(sides[2 * group + 1], x_pairs(1)) for group in range(2)]
    high = [send(sides[2 * group], x_pairs(-1)) for group in range(2)]
    inner = call(second_kernel, array(4, 8, K, K), [left_tables], 2 * 10**9)(v, tx, vx)
    pieces = [None] * 8
    for group, slots in enumerate(GROUPS):
        cut = call(functools.partial(second_edge_kernel, slots), [array(4, 8, 16, K)] * 4, mib=2)(
            inner, low[group], high[group], vx
        )
        for slot, piece in zip(slots, cut):
            pieces[slot] = send(piece, back(exchange_pairs(slot)))

    def by_x(*shape):
        return pl.BlockSpec((1, *shape), lambda x: (x, 0, 0, 0))

    return pl.pallas_call(
        final_kernel,
        grid=(4,),
        out_shape=array(4, 64, 16, K),
        in_specs=[by_x(64, 16, K)] + [by_x(8, 16, K)] * 8,
        out_specs=by_x(64, 16, K),
        compiler_params=params(),
        cost_estimate=cost(0, 6),
        name="final_kernel",
    )(local, *pieces)


def solution(mesh):
    in_specs = (P("gx", None, "ka", None), P("gx", None), P(), P("ka"), P(), P("ka"), P())
    out_specs = P("gx", None, "ka", None)
    return jax.shard_map(
        per_device, mesh=mesh, in_specs=in_specs, out_specs=out_specs, check_vma=False
    )
```

```python
import functools
import math

import jax
import jax.numpy as jnp
import numpy as np
from jax import lax
from jax.experimental import pallas as pl
from jax.experimental.pallas import tpu as pltpu
from jax.sharding import PartitionSpec as P


F32 = jnp.float32
BF16 = jnp.bfloat16
K = 128
AXES = ("gx", "ka")
SLOTS = [(2, 0), (2, 1), (1, 0), (1, 1), (3, 0), (3, 1), (0, 0), (0, 1)]
GROUPS = ((2, 3, 4, 5), (0, 1, 6, 7))
FIRST, SECOND = SLOTS.index((0, 0)), SLOTS.index((0, 1))
VMEM = pl.BlockSpec(memory_space=pltpu.VMEM)


def flat(x, y, z, core):
    return ((x * 4 + z % 4) * 2 + core) * 8 + y * 2 + z // 4


def place(block, part):
    x, low, core = block // 8, block // 2 % 4, block % 2
    half = part // 4
    y = part if half == 0 else 7 - part
    return flat(x, y, (low + 2 + 4 * (half ^ x % 2)) % 8, core)


def part_of(y, half):
    return y if half == 0 else 7 - y


def slot_part(ka, slot):
    dy, ds = SLOTS[slot]
    return part_of((ka // 2 + dy) % 4, (ka % 2) ^ ds)


def exchange_pairs(slot):
    return [
        (block * 8 + ka, place(block, slot_part(ka, slot)))
        for block in range(32)
        for ka in range(8)
    ]


def x_pairs(step):
    return [
        (place(block, part), place((block + step) % 32, part))
        for block in range(32)
        for part in range(8)
    ]


def y_pairs(step):
    return [
        (place(block, 4 * half + part), place(block, 4 * half + (part + step) % 4))
        for block in range(32)
        for half in range(2)
        for part in range(4)
    ]


def middle_pairs(y):
    return [
        (place(block, part_of(y, half)), place(block, part_of(3, half)))
        for block in range(32)
        for half in range(2)
    ]


def send(value, pairs):
    return lax.ppermute(value, AXES, pairs)


def as_source():
    ka = lax.axis_index("ka")
    return ka >> 1, ka & 1


def as_host():
    gx, ka = lax.axis_index("gx"), lax.axis_index("ka")
    z = (ka & 1) * 4 + ((gx >> 1) & 3)
    turn = (z - 2) & 7
    return ka >> 1, (turn >> 2) ^ ((gx >> 3) & 1), (gx & 25) + (turn & 3) * 2


def part_index(y, half):
    return y + half * (7 - 2 * y)


def rows_to(slot):
    y, half = as_source()
    dy, ds = SLOTS[slot]
    return pl.ds(pl.multiple_of(part_index((y + dy) & 3, half ^ ds) * 8, 8), 8)


def kx_of(slot):
    y, half, block = as_host()
    dy, ds = SLOTS[slot]
    return pl.ds(pl.multiple_of((((y - dy) & 3) * 2 + (half ^ ds)) * 16, 16), 16)


def send_all(pieces, pairs, after):
    came = {}
    for slot in (0, 1, 2, 6, 7, 3, 4, 5):
        piece = pieces[slot]
        if slot in after:
            piece, came[after[slot]] = lax.optimization_barrier((piece, came[after[slot]]))
        came[slot] = send(piece, pairs(slot))
    return [came[slot] for slot in range(8)]


def halves(value):
    high = value.astype(BF16)
    return high, (value - high.astype(F32)).astype(BF16)


def circulant(row):
    return pltpu.roll(jnp.broadcast_to(row, (K, K)), 0, 1, stride=1, stride_axis=0)


def right_table(row):
    high, low = halves(circulant(row))
    return jnp.concatenate(
        [
            jnp.concatenate([high, low], 1),
            jnp.concatenate([high, jnp.zeros_like(low)], 1),
        ],
        0,
    )


def left_table(row):
    high, low = halves(circulant(row))
    return jnp.concatenate(
        [
            jnp.concatenate([high, high], 1),
            jnp.concatenate([low, jnp.zeros_like(low)], 1),
        ],
        0,
    )


def times_right(rows, table):
    both = jnp.dot(jnp.concatenate(halves(rows), 1), table, preferred_element_type=F32)
    return both[:, :K] + both[:, K:]


def times_left(table, first, second):
    high_0, low_0 = halves(first)
    high_1, low_1 = halves(second)
    stacked = jnp.concatenate(
        [jnp.concatenate([high_0, high_1], 1), jnp.concatenate([low_0, low_1], 1)], 0
    )
    both = jnp.dot(table, stacked, preferred_element_type=F32)
    both = both[:K] + both[K:]
    return both[:, :K], both[:, K:]


def slope(center, one, two):
    return 3.0 * center - 4.0 * one + two


def local_kernel(g_ref, ty_ref, vy_ref, out_ref, pad):
    vy = vy_ref[...].reshape(1, 1, K)
    toward = jnp.broadcast_to(vy > 0, (4, 16, K))
    rate = jnp.abs(vy) * 0.125

    def step(value, one_low, two_low, one_high, two_high, table):
        one = jnp.where(toward, one_low, one_high)
        two = jnp.where(toward, two_low, two_high)
        wigner = times_right(value.reshape(64, K), table).reshape(4, 16, K)
        return wigner - rate * slope(value, one, two)

    edge = jnp.zeros((4, 2, 16, K), F32)
    pad[0, :, 0:2] = edge
    pad[0, :, 66:68] = edge
    pad[1, :, 0:2] = edge
    pad[1, :, 66:68] = edge
    for y in range(64):
        pad[0, :, y + 2] = g_ref[:, y]

    def turn(source, into):
        @pl.loop(0, 8)
        def _(group):
            block = ty_ref[pl.ds(pl.multiple_of(group * 8, 8), 8), :]
            for inner in range(8):
                y = group * 8 + inner
                value = pad[source, :, y + 2]
                moved = step(
                    value,
                    pad[source, :, y + 1],
                    pad[source, :, y],
                    pad[source, :, y + 3],
                    pad[source, :, y + 4],
                    right_table(block[inner : inner + 1]),
                )
                into(y, value, moved)

    def first(y, value, moved):
        pad[1, :, y + 2] = value + moved

    def second(y, value, moved):
        out_ref[:, y] = 0.5 * (pad[0, :, y + 2] + value + moved)

    turn(0, first)
    turn(1, second)


def pack_kernel(g_ref, vel_ref, potential_ref, *pieces):
    y, half = as_source()
    for slot in range(8):
        at = rows_to(slot)
        for x in range(4):
            pieces[slot][8 * x : 8 * x + 8] = g_ref[x, at]
        pieces[slot][32] = vel_ref[...]
        dy, ds = SLOTS[slot]
        if dy == 0:
            at = pl.ds(32 - 2 * (half ^ ds), 2)
            for x in range(4):
                pieces[slot][33 + 2 * x : 35 + 2 * x] = g_ref[x, at]
    pieces[FIRST][41, 0:4] = potential_ref[...]
    pieces[FIRST][41, 4:16] = jnp.zeros((12, K), F32)


def across_kernel(first_ref, second_ref, out_ref):
    out_ref[0] = first_ref[33:41]
    out_ref[1] = second_ref[33:41]


def cut_kernel(*refs):
    pieces, (head_ref, tail_ref, bottom_ref, top_ref) = refs[:8], refs[8:]
    for slot in range(8):
        head_ref[slot] = pieces[slot][0:16]
        tail_ref[slot] = pieces[slot][16:32]
        for x in range(4):
            bottom_ref[slot, 2 * x : 2 * x + 2] = pieces[slot][8 * x : 8 * x + 2]
            top_ref[slot, 2 * x : 2 * x + 2] = pieces[slot][8 * x + 6 : 8 * x + 8]


def inner_drift(center, x, layer, toward, rate):
    total = 3.0 * center
    for step, factor in ((1, -4.0), (2, 1.0)):
        low = layer(x - step) if x - step >= 0 else None
        high = layer(x + step) if x + step <= 3 else None
        if low is None:
            if high is not None:
                total += factor * jnp.where(toward, 0.0, high)
        elif high is None:
            total += factor * jnp.where(toward, low, 0.0)
        else:
            total += factor * jnp.where(toward, low, high)
    return -rate * total


def outer_drift(x, low, high, up, down):
    if x == 0:
        return up * (4.0 * low(0) - low(1))
    if x == 1:
        return -up * low(0)
    if x == 2:
        return -down * high(0)
    return down * (4.0 * high(0) - high(1))


def rates(vx_ref, at, factor):
    vx = vx_ref[at, :]
    block = as_host()[2]
    up = jnp.where(block == 0, 0.0, jnp.maximum(vx, 0.0) * factor)
    down = jnp.where(block == 31, 0.0, jnp.maximum(-vx, 0.0) * factor)
    return up[None], down[None]


def first_kernel(*refs):
    pieces, (sine_ref, ty_ref, vy_ref), (v_ref, vx_ref, tx_ref), (field, tables) = refs[:8], refs[8:11], refs[11:14], refs[14:]
    for slot in range(8):
        at = kx_of(slot)
        for x in range(4):
            field[x, :, at, :] = pieces[slot][8 * x : 8 * x + 8]
        vx_ref[at, :] = pieces[slot][32]
    tx_ref[...] = 0.25 * jnp.dot(
        pieces[FIRST][41, 0:8], sine_ref[...], precision=lax.Precision.HIGHEST, preferred_element_type=F32
    )
    for x in range(4):
        tables[x] = left_table(0.5 * tx_ref[x : x + 1, :])
    y_place, half, block = as_host()
    ty = ty_ref[pl.ds(pl.multiple_of(part_index(y_place, half) * 8, 8), 8), :]

    vx = vx_ref[...]
    toward = vx > 0
    rate = jnp.abs(vx) * 0.0625
    vy = jnp.broadcast_to(vy_ref[...], (K, K))
    toward_y = vy > 0
    rate_y = jnp.abs(vy) * 0.125
    zero = jnp.zeros((K, K), F32)
    for pair in range(4):
        right = [right_table(ty[pair * 2 + i : pair * 2 + i + 1, :]) for i in range(2)]
        for x in range(4):
            mine = [field[x, pair * 2 + i] for i in range(2)]
            wigner = times_left(tables[x], mine[0], mine[1])
            for i in range(2):
                y = pair * 2 + i
                total = mine[i] + wigner[i]
                total += inner_drift(mine[i], x, lambda at: field[at, y], toward, rate)
                total += times_right(mine[i], right[i])
                near = [field[x, at] if 0 <= at < 8 else zero for at in (y - 2, y - 1, y + 1, y + 2)]
                one = jnp.where(toward_y, near[1], near[2])
                two = jnp.where(toward_y, near[0], near[3])
                v_ref[x, y] = total - rate_y * slope(mine[i], one, two)


def first_edge_kernel(
    inner_ref, low_ref, high_ref, under_ref, over_ref, from_0_ref, from_1_ref, from_2_ref, own_0_ref, own_1_ref, vx_ref, vy_ref, v_ref, *outs
):
    y_place, half, block = as_host()
    middle = jnp.where(y_place == 3, 1.0, 0.0)
    under_middle, over_middle = y_place == 3 * half, y_place == 3 - 3 * half
    vy = vy_ref[...].reshape(1, 1, K)
    up_y = jnp.maximum(vy, 0.0) * 0.125
    down_y = jnp.maximum(-vy, 0.0) * 0.125

    def beside(ref, pair, rows):
        return ref[SLOTS.index(pair), rows]

    for slot in range(8):
        dy, ds = SLOTS[slot]
        at = kx_of(slot)
        up, down = rates(vx_ref, at, 0.0625)
        group = int(slot in GROUPS[1])
        i = GROUPS[group].index(slot)
        for x in range(4):
            rows = slice(2 * x, 2 * x + 2)
            if dy == 0:
                across = (own_0_ref, own_1_ref)[ds][33 + 2 * x : 35 + 2 * x]
            else:
                across = (from_2_ref, from_1_ref, from_0_ref)[dy - 1][ds, rows]
            before, after = ((dy + 3) % 4, ds), ((dy + 1) % 4, ds)
            under = jnp.where(half == 0, beside(under_ref, before, rows), beside(under_ref, after, rows))
            over = jnp.where(half == 0, beside(over_ref, after, rows), beside(over_ref, before, rows))
            under = jnp.where(under_middle, across * middle, under)
            over = jnp.where(over_middle, across * middle, over)
            value = inner_ref[x, :, at, :] + outer_drift(
                x,
                lambda n: low_ref[slot, 8 - 8 * n : 16 - 8 * n],
                lambda n: high_ref[slot, 8 * n : 8 * n + 8],
                up,
                down,
            )
            bottom = jnp.concatenate([up_y * (4.0 * under[1:2] - under[0:1]), -up_y * under[1:2]], 0)
            top = jnp.concatenate([-down_y * over[0:1], down_y * (4.0 * over[0:1] - over[1:2])], 0)
            value = jnp.concatenate([value[0:2] + bottom, value[2:6], value[6:8] + top], 0)
            v_ref[x, :, at, :] = value
            side = outs[2 * group + x // 2]
            side[i, 8 * (x % 2) : 8 * (x % 2) + 8] = value


def second_kernel(v_ref, tx_ref, vx_ref, out_ref, tables):
    for x in range(4):
        tables[x] = left_table(tx_ref[x : x + 1, :])

    @pl.loop(0, 4)
    def _(pair):
        vx = vx_ref[...]
        toward = vx > 0
        rate = jnp.abs(vx) * 0.125
        for x in range(4):
            mine = [v_ref[x, pair * 2 + i] for i in range(2)]
            wigner = times_left(tables[x], mine[0], mine[1])
            for i in range(2):
                y = pair * 2 + i
                out_ref[x, y] = wigner[i] + inner_drift(mine[i], x, lambda at: v_ref[at, y], toward, rate)


def second_edge_kernel(slots, inner_ref, low_ref, high_ref, vx_ref, *pieces):
    for i, slot in enumerate(slots):
        at = kx_of(slot)
        up, down = rates(vx_ref, at, 0.125)
        for x in range(4):
            pieces[i][x] = inner_ref[x, :, at, :] + outer_drift(
                x,
                lambda n: low_ref[i, 8 - 8 * n : 16 - 8 * n],
                lambda n: high_ref[i, 8 * n : 8 * n + 8],
                up,
                down,
            )


def final_kernel(local_ref, *refs):
    pieces, out_ref = refs[:8], refs[8]
    for slot in range(8):
        at = rows_to(slot)
        out_ref[:, at] = local_ref[:, at] + pieces[slot][...]


MIB = 1 << 20


def array(*shape):
    return jax.ShapeDtypeStruct(shape, F32)


def params():
    return pltpu.CompilerParams(vmem_limit_bytes=40 * MIB)


def cost(flops, mib):
    return pl.CostEstimate(flops=flops, bytes_accessed=mib * MIB, transcendentals=0)


def call(kernel, outs, scratch=(), flops=0, mib=4):
    def run(*operands):
        return pl.pallas_call(
            kernel,
            out_shape=outs,
            in_specs=[VMEM] * len(operands),
            out_specs=[VMEM] * len(outs) if isinstance(outs, list) else VMEM,
            scratch_shapes=list(scratch),
            compiler_params=params(),
            cost_estimate=cost(flops, mib),
            name=(kernel.func if isinstance(kernel, functools.partial) else kernel).__name__,
        )(*operands)

    return run


def sine_table(sign):
    index = np.arange(K)
    angle = (sign * index[:, None] * index[None, :] % K) * (2.0 * math.pi / K)
    return (np.sin(angle) / K).astype(np.float32)


def back(pairs):
    return [(there, here) for here, there in pairs]


def per_device(density, potential_x, potential_y, speeds_x, speeds_y, upwind_x, upwind_y):
    vel_x = (2 * upwind_x - 1).astype(F32) * speeds_x
    vel_x = jnp.broadcast_to(vel_x[:, None], (16, K))
    vy = ((2 * upwind_y - 1).astype(F32) * speeds_y).reshape(1, K)

    sizes = [33 + 8 * (dy == 0) + (slot == FIRST) for slot, (dy, ds) in enumerate(SLOTS)]
    pieces = call(pack_kernel, [array(size, 16, K) for size in sizes])(density, vel_x, potential_x)
    pieces = send_all(pieces, exchange_pairs, {3: 7, 4: 6, 5: 1})

    highest = lax.Precision.HIGHEST
    ty = 0.25 * jnp.dot(potential_y, jnp.asarray(sine_table(1)), precision=highest)
    local = call(
        local_kernel, array(4, 64, 16, K), [pltpu.VMEM((2, 4, 68, 16, K), F32)], 4 * 10**9
    )(density, ty, vy)

    across = call(across_kernel, array(2, 8, 16, K), mib=0)(pieces[FIRST], pieces[SECOND])
    across = [send(across, middle_pairs(y)) for y in range(3)]
    *pieces, across[0], across[1], across[2] = lax.optimization_barrier((*pieces, *across))
    head, tail, bottom, top = call(cut_kernel, [array(8, 16, 16, K)] * 2 + [array(8, 8, 16, K)] * 2)(*pieces)
    low, high = send(tail, x_pairs(1)), send(head, x_pairs(-1))
    under, over = send(top, y_pairs(1)), send(bottom, y_pairs(-1))
    left_tables = pltpu.VMEM((4, 2 * K, 2 * K), BF16)
    inner, vx, tx = call(
        first_kernel,
        [array(4, 8, K, K), array(K, K), array(8, K)],
        [pltpu.VMEM((4, 8, K, K), F32), left_tables],
        3 * 10**9,
    )(*pieces, jnp.asarray(sine_table(-1)), ty, vy)
    v, *sides = call(first_edge_kernel, [array(4, 8, K, K)] + [array(4, 16, 16, K)] * 4)(
        inner, low, high, under, over, *across, pieces[FIRST], pieces[SECOND], vx, vy
    )
    low = [send(sides[2 * group + 1], x_pairs(1)) for group in range(2)]
    high = [send(sides[2 * group], x_pairs(-1)) for group in range(2)]
    inner = call(second_kernel, array(4, 8, K, K), [left_tables], 2 * 10**9)(v, tx, vx)
    pieces = [None] * 8
    for group, slots in enumerate(GROUPS):
        cut = call(functools.partial(second_edge_kernel, slots), [array(4, 8, 16, K)] * 4, mib=2)(
            inner, low[group], high[group], vx
        )
        for slot, piece in zip(slots, cut):
            pieces[slot] = piece
    pieces = send_all(pieces, lambda slot: back(exchange_pairs(slot)), {3: 6, 4: 7, 5: 0})

    def by_x(*shape):
        return pl.BlockSpec((1, *shape), lambda x: (x, 0, 0, 0))

    return pl.pallas_call(
        final_kernel,
        grid=(4,),
        out_shape=array(4, 64, 16, K),
        in_specs=[by_x(64, 16, K)] + [by_x(8, 16, K)] * 8,
        out_specs=by_x(64, 16, K),
        compiler_params=params(),
        cost_estimate=cost(0, 6),
        name="final_kernel",
    )(local, *pieces)


def solution(mesh):
    in_specs = (P("gx", None, "ka", None), P("gx", None), P(), P("ka"), P(), P("ka"), P())
    out_specs = P("gx", None, "ka", None)
    return jax.shard_map(
        per_device, mesh=mesh, in_specs=in_specs, out_specs=out_specs, check_vma=False
    )
```

```python
import functools
import math

import jax
import jax.numpy as jnp
import numpy as np
from jax import lax
from jax.experimental import pallas as pl
from jax.experimental.pallas import tpu as pltpu
from jax.sharding import PartitionSpec as P


F32 = jnp.float32
BF16 = jnp.bfloat16
K = 128
AXES = ("gx", "ka")
SLOTS = [(2, 0), (2, 1), (1, 0), (1, 1), (3, 0), (3, 1), (0, 0), (0, 1)]
GROUPS = ((2, 3, 4, 5), (0, 1, 6, 7))
FIRST, SECOND = SLOTS.index((0, 0)), SLOTS.index((0, 1))
VMEM = pl.BlockSpec(memory_space=pltpu.VMEM)


def flat(x, y, z, core):
    return ((x * 4 + z % 4) * 2 + core) * 8 + y * 2 + z // 4


def place(block, part):
    x, low, core = block // 8, block // 2 % 4, block % 2
    half = part // 4
    y = part if half == 0 else 7 - part
    return flat(x, y, (low + 2 + 4 * (half ^ x % 2)) % 8, core)


def part_of(y, half):
    return y if half == 0 else 7 - y


def slot_part(ka, slot):
    dy, ds = SLOTS[slot]
    return part_of((ka // 2 + dy) % 4, (ka % 2) ^ ds)


def exchange_pairs(slot):
    return [
        (block * 8 + ka, place(block, slot_part(ka, slot)))
        for block in range(32)
        for ka in range(8)
    ]


def x_pairs(step):
    return [
        (place(block, part), place((block + step) % 32, part))
        for block in range(32)
        for part in range(8)
    ]


def y_pairs(step):
    return [
        (place(block, 4 * half + part), place(block, 4 * half + (part + step) % 4))
        for block in range(32)
        for half in range(2)
        for part in range(4)
    ]


def middle_pairs(y):
    return [
        (place(block, part_of(y, half)), place(block, part_of(3, half)))
        for block in range(32)
        for half in range(2)
    ]


def send(value, pairs):
    return lax.ppermute(value, AXES, pairs)


def as_source():
    ka = lax.axis_index("ka")
    return ka >> 1, ka & 1


def as_host():
    gx, ka = lax.axis_index("gx"), lax.axis_index("ka")
    z = (ka & 1) * 4 + ((gx >> 1) & 3)
    turn = (z - 2) & 7
    return ka >> 1, (turn >> 2) ^ ((gx >> 3) & 1), (gx & 25) + (turn & 3) * 2


def part_index(y, half):
    return y + half * (7 - 2 * y)


def rows_to(slot):
    y, half = as_source()
    dy, ds = SLOTS[slot]
    return pl.ds(pl.multiple_of(part_index((y + dy) & 3, half ^ ds) * 8, 8), 8)


def kx_of(slot):
    y, half, block = as_host()
    dy, ds = SLOTS[slot]
    return pl.ds(pl.multiple_of((((y - dy) & 3) * 2 + (half ^ ds)) * 16, 16), 16)


def send_all(pieces, pairs, after):
    came = {}
    for slot in (0, 1, 2, 6, 7, 3, 4, 5):
        piece = pieces[slot]
        if slot in after:
            piece, came[after[slot]] = lax.optimization_barrier((piece, came[after[slot]]))
        came[slot] = send(piece, pairs(slot))
    return [came[slot] for slot in range(8)]


def halves(value):
    high = value.astype(BF16)
    return high, (value - high.astype(F32)).astype(BF16)


def circulant(row):
    return pltpu.roll(jnp.broadcast_to(row, (K, K)), 0, 1, stride=1, stride_axis=0)


def right_table(row):
    high, low = halves(circulant(row))
    return jnp.concatenate(
        [
            jnp.concatenate([high, low], 1),
            jnp.concatenate([high, jnp.zeros_like(low)], 1),
        ],
        0,
    )


def left_table(row):
    high, low = halves(circulant(row))
    return jnp.concatenate(
        [
            jnp.concatenate([high, high], 1),
            jnp.concatenate([low, jnp.zeros_like(low)], 1),
        ],
        0,
    )


def times_right(rows, table):
    both = jnp.dot(jnp.concatenate(halves(rows), 1), table, preferred_element_type=F32)
    return both[:, :K] + both[:, K:]


def times_left(table, first, second):
    high_0, low_0 = halves(first)
    high_1, low_1 = halves(second)
    stacked = jnp.concatenate(
        [jnp.concatenate([high_0, high_1], 1), jnp.concatenate([low_0, low_1], 1)], 0
    )
    both = jnp.dot(table, stacked, preferred_element_type=F32)
    both = both[:K] + both[K:]
    return both[:, :K], both[:, K:]


def slope(center, one, two):
    return 3.0 * center - 4.0 * one + two


def local_kernel(g_ref, ty_ref, vy_ref, out_ref, pad):
    vy = vy_ref[...].reshape(1, 1, K)
    toward = jnp.broadcast_to(vy > 0, (4, 16, K))
    rate = jnp.abs(vy) * 0.125

    def step(value, one_low, two_low, one_high, two_high, table):
        one = jnp.where(toward, one_low, one_high)
        two = jnp.where(toward, two_low, two_high)
        wigner = times_right(value.reshape(64, K), table).reshape(4, 16, K)
        return wigner - rate * slope(value, one, two)

    edge = jnp.zeros((4, 2, 16, K), F32)
    pad[0, :, 0:2] = edge
    pad[0, :, 66:68] = edge
    pad[1, :, 0:2] = edge
    pad[1, :, 66:68] = edge
    for y in range(64):
        pad[0, :, y + 2] = g_ref[:, y]

    def turn(source, into):
        @pl.loop(0, 8)
        def _(group):
            block = ty_ref[pl.ds(pl.multiple_of(group * 8, 8), 8), :]
            for inner in range(8):
                y = group * 8 + inner
                value = pad[source, :, y + 2]
                moved = step(
                    value,
                    pad[source, :, y + 1],
                    pad[source, :, y],
                    pad[source, :, y + 3],
                    pad[source, :, y + 4],
                    right_table(block[inner : inner + 1]),
                )
                into(y, value, moved)

    def first(y, value, moved):
        pad[1, :, y + 2] = value + moved

    def second(y, value, moved):
        out_ref[:, y] = 0.5 * (pad[0, :, y + 2] + value + moved)

    turn(0, first)
    turn(1, second)


def pack_kernel(g_ref, vel_ref, potential_ref, *pieces):
    y, half = as_source()
    for slot in range(8):
        at = rows_to(slot)
        for x in range(4):
            pieces[slot][8 * x : 8 * x + 8] = g_ref[x, at]
        pieces[slot][32] = vel_ref[...]
        dy, ds = SLOTS[slot]
        if dy == 0:
            at = pl.ds(32 - 2 * (half ^ ds), 2)
            for x in range(4):
                pieces[slot][33 + 2 * x : 35 + 2 * x] = g_ref[x, at]
    pieces[FIRST][41, 0:4] = potential_ref[...]
    pieces[FIRST][41, 4:16] = jnp.zeros((12, K), F32)


def across_kernel(first_ref, second_ref, out_ref):
    out_ref[0] = first_ref[33:41]
    out_ref[1] = second_ref[33:41]


def cut_kernel(*refs):
    pieces, (head_ref, tail_ref, bottom_ref, top_ref) = refs[:8], refs[8:]
    for slot in range(8):
        head_ref[slot] = pieces[slot][0:16]
        tail_ref[slot] = pieces[slot][16:32]
        for x in range(4):
            bottom_ref[slot, 2 * x : 2 * x + 2] = pieces[slot][8 * x : 8 * x + 2]
            top_ref[slot, 2 * x : 2 * x + 2] = pieces[slot][8 * x + 6 : 8 * x + 8]


def inner_drift(center, x, layer, toward, rate):
    total = 3.0 * center
    for step, factor in ((1, -4.0), (2, 1.0)):
        low = layer(x - step) if x - step >= 0 else None
        high = layer(x + step) if x + step <= 3 else None
        if low is None:
            if high is not None:
                total += factor * jnp.where(toward, 0.0, high)
        elif high is None:
            total += factor * jnp.where(toward, low, 0.0)
        else:
            total += factor * jnp.where(toward, low, high)
    return -rate * total


def outer_drift(x, low, high, up, down):
    if x == 0:
        return up * (4.0 * low(0) - low(1))
    if x == 1:
        return -up * low(0)
    if x == 2:
        return -down * high(0)
    return down * (4.0 * high(0) - high(1))


def rates(vx_ref, at, factor):
    vx = vx_ref[at, :]
    block = as_host()[2]
    up = jnp.where(block == 0, 0.0, jnp.maximum(vx, 0.0) * factor)
    down = jnp.where(block == 31, 0.0, jnp.maximum(-vx, 0.0) * factor)
    return up[None], down[None]


def first_kernel(*refs):
    pieces, (sine_ref, ty_ref, vy_ref), (v_ref, vx_ref, tx_ref), (field, tables) = refs[:8], refs[8:11], refs[11:14], refs[14:]
    for slot in range(8):
        at = kx_of(slot)
        for x in range(4):
            field[x, :, at, :] = pieces[slot][8 * x : 8 * x + 8]
        vx_ref[at, :] = pieces[slot][32]
    tx_ref[...] = 0.25 * jnp.dot(
        pieces[FIRST][41, 0:8], sine_ref[...], precision=lax.Precision.HIGHEST, preferred_element_type=F32
    )
    for x in range(4):
        tables[x] = left_table(0.5 * tx_ref[x : x + 1, :])
    y_place, half, block = as_host()
    ty = ty_ref[pl.ds(pl.multiple_of(part_index(y_place, half) * 8, 8), 8), :]

    vx = vx_ref[...]
    toward = vx > 0
    rate = jnp.abs(vx) * 0.0625
    vy = jnp.broadcast_to(vy_ref[...], (K, K))
    toward_y = vy > 0
    rate_y = jnp.abs(vy) * 0.125
    zero = jnp.zeros((K, K), F32)
    for pair in range(4):
        right = [right_table(ty[pair * 2 + i : pair * 2 + i + 1, :]) for i in range(2)]
        for x in range(4):
            mine = [field[x, pair * 2 + i] for i in range(2)]
            wigner = times_left(tables[x], mine[0], mine[1])
            for i in range(2):
                y = pair * 2 + i
                total = mine[i] + wigner[i]
                total += inner_drift(mine[i], x, lambda at: field[at, y], toward, rate)
                total += times_right(mine[i], right[i])
                near = [field[x, at] if 0 <= at < 8 else zero for at in (y - 2, y - 1, y + 1, y + 2)]
                one = jnp.where(toward_y, near[1], near[2])
                two = jnp.where(toward_y, near[0], near[3])
                v_ref[x, y] = total - rate_y * slope(mine[i], one, two)


def first_edge_kernel(
    inner_ref, under_ref, over_ref, low_ref, high_ref, from_0_ref, from_1_ref, from_2_ref, own_0_ref, own_1_ref, vx_ref, vy_ref, v_ref, *outs
):
    y_place, half, block = as_host()
    middle = jnp.where(y_place == 3, 1.0, 0.0)
    under_middle, over_middle = y_place == 3 * half, y_place == 3 - 3 * half
    vy = vy_ref[...].reshape(1, 1, K)
    up_y = jnp.maximum(vy, 0.0) * 0.125
    down_y = jnp.maximum(-vy, 0.0) * 0.125

    def beside(ref, pair, rows):
        return ref[SLOTS.index(pair), rows]

    for slot in range(8):
        dy, ds = SLOTS[slot]
        at = kx_of(slot)
        up, down = rates(vx_ref, at, 0.0625)
        group = int(slot in GROUPS[1])
        i = GROUPS[group].index(slot)
        for x in range(4):
            rows = slice(2 * x, 2 * x + 2)
            if dy == 0:
                across = (own_0_ref, own_1_ref)[ds][33 + 2 * x : 35 + 2 * x]
            else:
                across = (from_2_ref, from_1_ref, from_0_ref)[dy - 1][ds, rows]
            before, after = ((dy + 3) % 4, ds), ((dy + 1) % 4, ds)
            under = jnp.where(half == 0, beside(under_ref, before, rows), beside(under_ref, after, rows))
            over = jnp.where(half == 0, beside(over_ref, after, rows), beside(over_ref, before, rows))
            under = jnp.where(under_middle, across * middle, under)
            over = jnp.where(over_middle, across * middle, over)
            value = inner_ref[x, :, at, :] + outer_drift(
                x,
                lambda n: low_ref[slot, 8 - 8 * n : 16 - 8 * n],
                lambda n: high_ref[slot, 8 * n : 8 * n + 8],
                up,
                down,
            )
            bottom = jnp.concatenate([up_y * (4.0 * under[1:2] - under[0:1]), -up_y * under[1:2]], 0)
            top = jnp.concatenate([-down_y * over[0:1], down_y * (4.0 * over[0:1] - over[1:2])], 0)
            value = jnp.concatenate([value[0:2] + bottom, value[2:6], value[6:8] + top], 0)
            v_ref[x, :, at, :] = value
            side = outs[2 * group + x // 2]
            side[i, 8 * (x % 2) : 8 * (x % 2) + 8] = value


def second_kernel(v_ref, tx_ref, vx_ref, out_ref, tables):
    for x in range(4):
        tables[x] = left_table(tx_ref[x : x + 1, :])

    @pl.loop(0, 4)
    def _(pair):
        vx = vx_ref[...]
        toward = vx > 0
        rate = jnp.abs(vx) * 0.125
        for x in range(4):
            mine = [v_ref[x, pair * 2 + i] for i in range(2)]
            wigner = times_left(tables[x], mine[0], mine[1])
            for i in range(2):
                y = pair * 2 + i
                out_ref[x, y] = wigner[i] + inner_drift(mine[i], x, lambda at: v_ref[at, y], toward, rate)


def second_edge_kernel(slots, inner_ref, low_ref, high_ref, vx_ref, *pieces):
    for i, slot in enumerate(slots):
        at = kx_of(slot)
        up, down = rates(vx_ref, at, 0.125)
        for x in range(4):
            pieces[i][x] = inner_ref[x, :, at, :] + outer_drift(
                x,
                lambda n: low_ref[i, 8 - 8 * n : 16 - 8 * n],
                lambda n: high_ref[i, 8 * n : 8 * n + 8],
                up,
                down,
            )


def final_kernel(local_ref, *refs):
    pieces, out_ref = refs[:8], refs[8]
    for slot in range(8):
        at = rows_to(slot)
        out_ref[:, at] = local_ref[:, at] + pieces[slot][...]


MIB = 1 << 20


def array(*shape):
    return jax.ShapeDtypeStruct(shape, F32)


def params():
    return pltpu.CompilerParams(vmem_limit_bytes=40 * MIB)


def cost(flops, mib):
    return pl.CostEstimate(flops=flops, bytes_accessed=mib * MIB, transcendentals=0)


def call(kernel, outs, scratch=(), flops=0, mib=4):
    def run(*operands):
        return pl.pallas_call(
            kernel,
            out_shape=outs,
            in_specs=[VMEM] * len(operands),
            out_specs=[VMEM] * len(outs) if isinstance(outs, list) else VMEM,
            scratch_shapes=list(scratch),
            compiler_params=params(),
            cost_estimate=cost(flops, mib),
            name=(kernel.func if isinstance(kernel, functools.partial) else kernel).__name__,
        )(*operands)

    return run


def sine_table(sign):
    index = np.arange(K)
    angle = (sign * index[:, None] * index[None, :] % K) * (2.0 * math.pi / K)
    return (np.sin(angle) / K).astype(np.float32)


def back(pairs):
    return [(there, here) for here, there in pairs]


def per_device(density, potential_x, potential_y, speeds_x, speeds_y, upwind_x, upwind_y):
    vel_x = (2 * upwind_x - 1).astype(F32) * speeds_x
    vel_x = jnp.broadcast_to(vel_x[:, None], (16, K))
    vy = ((2 * upwind_y - 1).astype(F32) * speeds_y).reshape(1, K)

    sizes = [33 + 8 * (dy == 0) + (slot == FIRST) for slot, (dy, ds) in enumerate(SLOTS)]
    pieces = call(pack_kernel, [array(size, 16, K) for size in sizes])(density, vel_x, potential_x)
    pieces = send_all(pieces, exchange_pairs, {3: 7, 4: 6, 5: 7})

    highest = lax.Precision.HIGHEST
    ty = 0.25 * jnp.dot(potential_y, jnp.asarray(sine_table(1)), precision=highest)
    local = call(
        local_kernel, array(4, 64, 16, K), [pltpu.VMEM((2, 4, 68, 16, K), F32)], 4 * 10**9
    )(density, ty, vy)

    across = call(across_kernel, array(2, 8, 16, K), mib=0)(pieces[FIRST], pieces[SECOND])
    across = [send(across, middle_pairs(y)) for y in range(3)]
    *pieces, across[0], across[1], across[2] = lax.optimization_barrier((*pieces, *across))
    head, tail, bottom, top = call(cut_kernel, [array(8, 16, 16, K)] * 2 + [array(8, 8, 16, K)] * 2)(*pieces)
    low, high = send(tail, x_pairs(1)), send(head, x_pairs(-1))
    under, over = send(top, y_pairs(1)), send(bottom, y_pairs(-1))
    left_tables = pltpu.VMEM((4, 2 * K, 2 * K), BF16)
    inner, vx, tx = call(
        first_kernel,
        [array(4, 8, K, K), array(K, K), array(8, K)],
        [pltpu.VMEM((4, 8, K, K), F32), left_tables],
        3 * 10**9,
    )(*pieces, jnp.asarray(sine_table(-1)), ty, vy)
    v, *sides = call(first_edge_kernel, [array(4, 8, K, K)] + [array(4, 16, 16, K)] * 4)(
        inner, under, over, low, high, *across, pieces[FIRST], pieces[SECOND], vx, vy
    )
    low = [send(sides[2 * group + 1], x_pairs(1)) for group in range(2)]
    high = [send(sides[2 * group], x_pairs(-1)) for group in range(2)]
    inner = call(second_kernel, array(4, 8, K, K), [left_tables], 2 * 10**9)(v, tx, vx)
    pieces = [None] * 8
    for group, slots in enumerate(GROUPS):
        cut = call(functools.partial(second_edge_kernel, slots), [array(4, 8, 16, K)] * 4, mib=2)(
            inner, low[group], high[group], vx
        )
        for slot, piece in zip(slots, cut):
            pieces[slot] = piece
    pieces = send_all(pieces, lambda slot: back(exchange_pairs(slot)), {})

    def by_x(*shape):
        return pl.BlockSpec((1, *shape), lambda x: (x, 0, 0, 0))

    return pl.pallas_call(
        final_kernel,
        grid=(4,),
        out_shape=array(4, 64, 16, K),
        in_specs=[by_x(64, 16, K)] + [by_x(8, 16, K)] * 8,
        out_specs=by_x(64, 16, K),
        compiler_params=params(),
        cost_estimate=cost(0, 6),
        name="final_kernel",
    )(local, *pieces)


def solution(mesh):
    in_specs = (P("gx", None, "ka", None), P("gx", None), P(), P("ka"), P(), P("ka"), P())
    out_specs = P("gx", None, "ka", None)
    return jax.shard_map(
        per_device, mesh=mesh, in_specs=in_specs, out_specs=out_specs, check_vma=False
    )
```

```python
import functools
import math

import jax
import jax.numpy as jnp
import numpy as np
from jax import lax
from jax.experimental import pallas as pl
from jax.experimental.pallas import tpu as pltpu
from jax.sharding import PartitionSpec as P


F32 = jnp.float32
BF16 = jnp.bfloat16
K = 128
AXES = ("gx", "ka")
SLOTS = [(2, 0), (2, 1), (1, 0), (1, 1), (3, 0), (3, 1), (0, 0), (0, 1)]
GROUPS = ((2, 3, 4, 5), (0, 1, 6, 7))
FIRST, SECOND = SLOTS.index((0, 0)), SLOTS.index((0, 1))
VMEM = pl.BlockSpec(memory_space=pltpu.VMEM)
HBM = pl.BlockSpec(memory_space=pltpu.HBM)


def flat(x, y, z, core):
    return ((x * 4 + z % 4) * 2 + core) * 8 + y * 2 + z // 4


def place(block, part):
    x, low, core = block // 8, block // 2 % 4, block % 2
    half = part // 4
    y = part if half == 0 else 7 - part
    return flat(x, y, (low + 2 + 4 * (half ^ x % 2)) % 8, core)


def part_of(y, half):
    return y if half == 0 else 7 - y


def slot_part(ka, slot):
    dy, ds = SLOTS[slot]
    return part_of((ka // 2 + dy) % 4, (ka % 2) ^ ds)


def exchange_pairs(slot):
    return [
        (block * 8 + ka, place(block, slot_part(ka, slot)))
        for block in range(32)
        for ka in range(8)
    ]


def x_pairs(odd):
    return [
        (place(block, part), place((block + (1 if block % 2 == odd else -1)) % 32, part))
        for block in range(32)
        for part in range(8)
    ]


def y_pairs(step):
    return [
        (place(block, 4 * half + part), place(block, 4 * half + (part + step) % 4))
        for block in range(32)
        for half in range(2)
        for part in range(4)
    ]


def middle_pairs(y):
    return [
        (place(block, part_of(y, half)), place(block, part_of(3, half)))
        for block in range(32)
        for half in range(2)
    ]


def send(value, pairs):
    return lax.ppermute(value, AXES, pairs)


def as_source():
    ka = lax.axis_index("ka")
    return ka >> 1, ka & 1


def as_host():
    gx, ka = lax.axis_index("gx"), lax.axis_index("ka")
    z = (ka & 1) * 4 + ((gx >> 1) & 3)
    turn = (z - 2) & 7
    return ka >> 1, (turn >> 2) ^ ((gx >> 3) & 1), (gx & 25) + (turn & 3) * 2


def part_index(y, half):
    return y + half * (7 - 2 * y)


def rows_to(slot):
    y, half = as_source()
    dy, ds = SLOTS[slot]
    return pl.ds(pl.multiple_of(part_index((y + dy) & 3, half ^ ds) * 8, 8), 8)


def kx_of(slot):
    y, half, block = as_host()
    dy, ds = SLOTS[slot]
    return pl.ds(pl.multiple_of((((y - dy) & 3) * 2 + (half ^ ds)) * 16, 16), 16)


def send_all(pieces, pairs, after):
    came = {}
    for slot in (0, 1, 2, 6, 7, 3, 4, 5):
        piece = pieces[slot]
        if slot in after:
            piece, came[after[slot]] = lax.optimization_barrier((piece, came[after[slot]]))
        came[slot] = send(piece, pairs(slot))
    return [came[slot] for slot in range(8)]


def halves(value):
    high = value.astype(BF16)
    return high, (value - high.astype(F32)).astype(BF16)


def circulant(row):
    return pltpu.roll(jnp.broadcast_to(row, (K, K)), 0, 1, stride=1, stride_axis=0)


def right_table(row):
    high, low = halves(circulant(row))
    return jnp.concatenate(
        [
            jnp.concatenate([high, low], 1),
            jnp.concatenate([high, jnp.zeros_like(low)], 1),
        ],
        0,
    )


def left_table(row):
    high, low = halves(circulant(row))
    return jnp.concatenate(
        [
            jnp.concatenate([high, high], 1),
            jnp.concatenate([low, jnp.zeros_like(low)], 1),
        ],
        0,
    )


def times_right(rows, table):
    both = jnp.dot(jnp.concatenate(halves(rows), 1), table, preferred_element_type=F32)
    return both[:, :K] + both[:, K:]


def times_left(table, first, second):
    high_0, low_0 = halves(first)
    high_1, low_1 = halves(second)
    stacked = jnp.concatenate(
        [jnp.concatenate([high_0, high_1], 1), jnp.concatenate([low_0, low_1], 1)], 0
    )
    both = jnp.dot(table, stacked, preferred_element_type=F32)
    both = both[:K] + both[K:]
    return both[:, :K], both[:, K:]


def slope(center, one, two):
    return 3.0 * center - 4.0 * one + two


def local_kernel(g_ref, ty_ref, vy_ref, out_ref, pad):
    vy = vy_ref[...].reshape(1, 1, K)
    toward = jnp.broadcast_to(vy > 0, (4, 16, K))
    rate = jnp.abs(vy) * 0.125

    def step(value, one_low, two_low, one_high, two_high, table):
        one = jnp.where(toward, one_low, one_high)
        two = jnp.where(toward, two_low, two_high)
        wigner = times_right(value.reshape(64, K), table).reshape(4, 16, K)
        return wigner - rate * slope(value, one, two)

    edge = jnp.zeros((4, 2, 16, K), F32)
    pad[0, :, 0:2] = edge
    pad[0, :, 66:68] = edge
    pad[1, :, 0:2] = edge
    pad[1, :, 66:68] = edge
    for y in range(64):
        pad[0, :, y + 2] = g_ref[:, y]

    def turn(source, into):
        @pl.loop(0, 8)
        def _(group):
            block = ty_ref[pl.ds(pl.multiple_of(group * 8, 8), 8), :]
            for inner in range(8):
                y = group * 8 + inner
                value = pad[source, :, y + 2]
                moved = step(
                    value,
                    pad[source, :, y + 1],
                    pad[source, :, y],
                    pad[source, :, y + 3],
                    pad[source, :, y + 4],
                    right_table(block[inner : inner + 1]),
                )
                into(y, value, moved)

    def first(y, value, moved):
        pad[1, :, y + 2] = value + moved

    def second(y, value, moved):
        out_ref[:, y] = 0.5 * (pad[0, :, y + 2] + value + moved)

    turn(0, first)
    turn(1, second)


def pack_kernel(g_ref, vel_ref, potential_ref, *pieces):
    y, half = as_source()
    for slot in range(8):
        at = rows_to(slot)
        for x in range(4):
            pieces[slot][8 * x : 8 * x + 8] = g_ref[x, at]
        pieces[slot][32] = vel_ref[...]
        dy, ds = SLOTS[slot]
        if dy == 0:
            at = pl.ds(32 - 2 * (half ^ ds), 2)
            for x in range(4):
                pieces[slot][33 + 2 * x : 35 + 2 * x] = g_ref[x, at]
    pieces[FIRST][41, 0:4] = potential_ref[...]
    pieces[FIRST][41, 4:16] = jnp.zeros((12, K), F32)


def across_kernel(first_ref, second_ref, out_ref):
    out_ref[0] = first_ref[33:41]
    out_ref[1] = second_ref[33:41]


def cut_kernel(*refs):
    pieces, (away_ref, near_ref, bottom_ref, top_ref) = refs[:8], refs[8:]
    core = lax.axis_index("gx") & 1
    for slot in range(8):
        away_ref[slot] = pieces[slot][pl.ds(core * 16, 16)]
        near_ref[slot] = pieces[slot][pl.ds(16 - core * 16, 16)]
        for x in range(4):
            bottom_ref[slot, 2 * x : 2 * x + 2] = pieces[slot][8 * x : 8 * x + 2]
            top_ref[slot, 2 * x : 2 * x + 2] = pieces[slot][8 * x + 6 : 8 * x + 8]


def inner_drift(center, x, layer, toward, rate):
    total = 3.0 * center
    for step, factor in ((1, -4.0), (2, 1.0)):
        low = layer(x - step) if x - step >= 0 else None
        high = layer(x + step) if x + step <= 3 else None
        if low is None:
            if high is not None:
                total += factor * jnp.where(toward, 0.0, high)
        elif high is None:
            total += factor * jnp.where(toward, low, 0.0)
        else:
            total += factor * jnp.where(toward, low, high)
    return -rate * total


def outer_drift(x, low, high, up, down):
    if x == 0:
        return up * (4.0 * low(0) - low(1))
    if x == 1:
        return -up * low(0)
    if x == 2:
        return -down * high(0)
    return down * (4.0 * high(0) - high(1))


def rates(vx_ref, at, factor):
    vx = vx_ref[at, :]
    block = as_host()[2]
    up = jnp.where(block == 0, 0.0, jnp.maximum(vx, 0.0) * factor)
    down = jnp.where(block == 31, 0.0, jnp.maximum(-vx, 0.0) * factor)
    return up[None], down[None]


def outer_layers(away_ref, near_ref, i):
    even = (lax.axis_index("gx") & 1) == 0

    def low(n):
        at = slice(8 - 8 * n, 16 - 8 * n)
        return jnp.where(even, away_ref[i, at], near_ref[i, at])

    def high(n):
        at = slice(8 * n, 8 * n + 8)
        return jnp.where(even, near_ref[i, at], away_ref[i, at])

    return low, high


def first_kernel(*refs):
    pieces, (sine_ref, ty_ref, vy_ref), (v_ref, vx_ref, tx_ref), (field, tables) = refs[:8], refs[8:11], refs[11:14], refs[14:]
    for slot in range(8):
        at = kx_of(slot)
        for x in range(4):
            field[x, :, at, :] = pieces[slot][8 * x : 8 * x + 8]
        vx_ref[at, :] = pieces[slot][32]
    tx_ref[...] = 0.25 * jnp.dot(
        pieces[FIRST][41, 0:8], sine_ref[...], precision=lax.Precision.HIGHEST, preferred_element_type=F32
    )
    for x in range(4):
        tables[x] = left_table(0.5 * tx_ref[x : x + 1, :])
    y_place, half, block = as_host()
    ty = ty_ref[pl.ds(pl.multiple_of(part_index(y_place, half) * 8, 8), 8), :]

    vx = vx_ref[...]
    toward = vx > 0
    rate = jnp.abs(vx) * 0.0625
    vy = jnp.broadcast_to(vy_ref[...], (K, K))
    toward_y = vy > 0
    rate_y = jnp.abs(vy) * 0.125
    zero = jnp.zeros((K, K), F32)
    for pair in range(4):
        right = [right_table(ty[pair * 2 + i : pair * 2 + i + 1, :]) for i in range(2)]
        for x in range(4):
            mine = [field[x, pair * 2 + i] for i in range(2)]
            wigner = times_left(tables[x], mine[0], mine[1])
            for i in range(2):
                y = pair * 2 + i
                total = mine[i] + wigner[i]
                total += inner_drift(mine[i], x, lambda at: field[at, y], toward, rate)
                total += times_right(mine[i], right[i])
                near = [field[x, at] if 0 <= at < 8 else zero for at in (y - 2, y - 1, y + 1, y + 2)]
                one = jnp.where(toward_y, near[1], near[2])
                two = jnp.where(toward_y, near[0], near[3])
                v_ref[x, y] = total - rate_y * slope(mine[i], one, two)


def first_edge_kernel(
    inner_ref, away_ref, near_ref, under_ref, over_ref, from_0_ref, from_1_ref, from_2_ref, own_0_ref, own_1_ref, vx_ref, vy_ref, v_ref, *outs
):
    y_place, half, block = as_host()
    middle = jnp.where(y_place == 3, 1.0, 0.0)
    under_middle, over_middle = y_place == 3 * half, y_place == 3 - 3 * half
    vy = vy_ref[...].reshape(1, 1, K)
    up_y = jnp.maximum(vy, 0.0) * 0.125
    down_y = jnp.maximum(-vy, 0.0) * 0.125

    def beside(ref, pair, rows):
        return ref[SLOTS.index(pair), rows]

    for slot in range(8):
        dy, ds = SLOTS[slot]
        at = kx_of(slot)
        up, down = rates(vx_ref, at, 0.0625)
        group = int(slot in GROUPS[1])
        i = GROUPS[group].index(slot)
        low, high = outer_layers(away_ref, near_ref, slot)
        even = (lax.axis_index("gx") & 1) == 0
        layers = []
        for x in range(4):
            rows = slice(2 * x, 2 * x + 2)
            if dy == 0:
                across = (own_0_ref, own_1_ref)[ds][33 + 2 * x : 35 + 2 * x]
            else:
                across = (from_2_ref, from_1_ref, from_0_ref)[dy - 1][ds, rows]
            before, after = ((dy + 3) % 4, ds), ((dy + 1) % 4, ds)
            under = jnp.where(half == 0, beside(under_ref, before, rows), beside(under_ref, after, rows))
            over = jnp.where(half == 0, beside(over_ref, after, rows), beside(over_ref, before, rows))
            under = jnp.where(under_middle, across * middle, under)
            over = jnp.where(over_middle, across * middle, over)
            value = inner_ref[x, :, at, :] + outer_drift(x, low, high, up, down)
            bottom = jnp.concatenate([up_y * (4.0 * under[1:2] - under[0:1]), -up_y * under[1:2]], 0)
            top = jnp.concatenate([-down_y * over[0:1], down_y * (4.0 * over[0:1] - over[1:2])], 0)
            value = jnp.concatenate([value[0:2] + bottom, value[2:6], value[6:8] + top], 0)
            v_ref[x, :, at, :] = value
            layers.append(value)
        near_out, away_out = outs[2 * group : 2 * group + 2]
        for x in range(2):
            at = slice(8 * x, 8 * x + 8)
            away_out[i, at] = jnp.where(even, layers[x], layers[x + 2])
            near_out[i, at] = jnp.where(even, layers[x + 2], layers[x])


def second_kernel(v_ref, tx_ref, vx_ref, out_ref, tables):
    for x in range(4):
        tables[x] = left_table(tx_ref[x : x + 1, :])

    @pl.loop(0, 4)
    def _(pair):
        vx = vx_ref[...]
        toward = vx > 0
        rate = jnp.abs(vx) * 0.125
        for x in range(4):
            mine = [v_ref[x, pair * 2 + i] for i in range(2)]
            wigner = times_left(tables[x], mine[0], mine[1])
            for i in range(2):
                y = pair * 2 + i
                out_ref[x, y] = wigner[i] + inner_drift(mine[i], x, lambda at: v_ref[at, y], toward, rate)


def second_edge_kernel(slots, inner_ref, away_ref, near_ref, vx_ref, *pieces):
    for i, slot in enumerate(slots):
        at = kx_of(slot)
        up, down = rates(vx_ref, at, 0.125)
        low, high = outer_layers(away_ref, near_ref, i)
        for x in range(4):
            pieces[i][x] = inner_ref[x, :, at, :] + outer_drift(x, low, high, up, down)


def final_kernel(local_ref, *refs):
    pieces, (out_ref, total, sems) = refs[:8], refs[8:]
    copies = []
    for x in range(4):
        for slot in range(8):
            at = rows_to(slot)
            total[x, at] = local_ref[x, at] + pieces[slot][x]
        copies.append(pltpu.make_async_copy(total.at[x], out_ref.at[x], sems.at[x]))
        copies[-1].start()
    for copy in copies:
        copy.wait()


MIB = 1 << 20


def array(*shape):
    return jax.ShapeDtypeStruct(shape, F32)


def params():
    return pltpu.CompilerParams(vmem_limit_bytes=40 * MIB)


def cost(flops, mib):
    return pl.CostEstimate(flops=flops, bytes_accessed=mib * MIB, transcendentals=0)


def call(kernel, outs, scratch=(), flops=0, mib=4, ins=None, out_specs=None):
    def run(*operands):
        return pl.pallas_call(
            kernel,
            out_shape=outs,
            in_specs=ins or [VMEM] * len(operands),
            out_specs=out_specs or ([VMEM] * len(outs) if isinstance(outs, list) else VMEM),
            scratch_shapes=list(scratch),
            compiler_params=params(),
            cost_estimate=cost(flops, mib),
            name=kernel.func.__name__ if isinstance(kernel, functools.partial) else kernel.__name__,
        )(*operands)

    return run


def sine_table(sign):
    index = np.arange(K)
    angle = (sign * index[:, None] * index[None, :] % K) * (2.0 * math.pi / K)
    return (np.sin(angle) / K).astype(np.float32)


def back(pairs):
    return [(there, here) for here, there in pairs]


def per_device(density, potential_x, potential_y, speeds_x, speeds_y, upwind_x, upwind_y):
    vel_x = (2 * upwind_x - 1).astype(F32) * speeds_x
    vel_x = jnp.broadcast_to(vel_x[:, None], (16, K))
    vy = ((2 * upwind_y - 1).astype(F32) * speeds_y).reshape(1, K)

    sizes = [33 + 8 * (dy == 0) + (slot == FIRST) for slot, (dy, ds) in enumerate(SLOTS)]
    pieces = call(pack_kernel, [array(size, 16, K) for size in sizes])(density, vel_x, potential_x)
    pieces = send_all(pieces, exchange_pairs, {3: 7, 4: 6, 5: 1})

    highest = lax.Precision.HIGHEST
    ty = 0.25 * jnp.dot(potential_y, jnp.asarray(sine_table(1)), precision=highest)
    local = call(
        local_kernel, array(4, 64, 16, K), [pltpu.VMEM((2, 4, 68, 16, K), F32)], 4 * 10**9
    )(density, ty, vy)

    across = call(across_kernel, array(2, 8, 16, K), mib=0)(pieces[FIRST], pieces[SECOND])
    across = [send(across, middle_pairs(y)) for y in range(3)]
    *pieces, across[0], across[1], across[2] = lax.optimization_barrier((*pieces, *across))
    away, near, bottom, top = call(cut_kernel, [array(8, 16, 16, K)] * 2 + [array(8, 8, 16, K)] * 2)(*pieces)
    near, away = send(near, x_pairs(0)), send(away, x_pairs(1))
    under, over = send(top, y_pairs(1)), send(bottom, y_pairs(-1))
    left_tables = pltpu.VMEM((4, 2 * K, 2 * K), BF16)
    inner, vx, tx = call(
        first_kernel,
        [array(4, 8, K, K), array(K, K), array(8, K)],
        [pltpu.VMEM((4, 8, K, K), F32), left_tables],
        3 * 10**9,
    )(*pieces, jnp.asarray(sine_table(-1)), ty, vy)
    v, *sides = call(first_edge_kernel, [array(4, 8, K, K)] + [array(4, 16, 16, K)] * 4)(
        inner, away, near, under, over, *across, pieces[FIRST], pieces[SECOND], vx, vy
    )
    away = [send(sides[2 * group + 1], x_pairs(1)) for group in range(2)]
    near = [send(sides[2 * group], x_pairs(0)) for group in range(2)]
    inner = call(second_kernel, array(4, 8, K, K), [left_tables], 2 * 10**9)(v, tx, vx)
    pieces = [None] * 8
    for group, slots in enumerate(GROUPS):
        cut = call(functools.partial(second_edge_kernel, slots), [array(4, 8, 16, K)] * 4, mib=2)(
            inner, away[group], near[group], vx
        )
        for slot, piece in zip(slots, cut):
            pieces[slot] = piece
    pieces = send_all(pieces, lambda slot: back(exchange_pairs(slot)), {3: 6, 4: 7, 5: 0})

    return call(
        final_kernel,
        array(4, 64, 16, K),
        [pltpu.VMEM((4, 64, 16, K), F32), pltpu.SemaphoreType.DMA((4,))],
        out_specs=HBM,
    )(local, *pieces)


def solution(mesh):
    in_specs = (P("gx", None, "ka", None), P("gx", None), P(), P("ka"), P(), P("ka"), P())
    out_specs = P("gx", None, "ka", None)
    return jax.shard_map(
        per_device, mesh=mesh, in_specs=in_specs, out_specs=out_specs, check_vma=False
    )
```

```python
import functools
import math

import jax
import jax.numpy as jnp
import numpy as np
from jax import lax
from jax.experimental import pallas as pl
from jax.experimental.pallas import tpu as pltpu
from jax.sharding import PartitionSpec as P


F32 = jnp.float32
BF16 = jnp.bfloat16
K = 128
AXES = ("gx", "ka")
SLOTS = [(2, 0), (2, 1), (1, 0), (1, 1), (3, 0), (3, 1), (0, 0), (0, 1)]
GROUPS = ((2, 3, 4, 5), (0, 1, 6, 7))
FIRST, SECOND = SLOTS.index((0, 0)), SLOTS.index((0, 1))
VMEM = pl.BlockSpec(memory_space=pltpu.VMEM)
HBM = pl.BlockSpec(memory_space=pltpu.HBM)


def flat(x, y, z, core):
    return ((x * 4 + z % 4) * 2 + core) * 8 + y * 2 + z // 4


def place(block, part):
    x, low, core = block // 8, block // 2 % 4, block % 2
    half = part // 4
    y = part if half == 0 else 7 - part
    return flat(x, y, (low + 2 + 4 * (half ^ x % 2)) % 8, core)


def part_of(y, half):
    return y if half == 0 else 7 - y


def slot_part(ka, slot):
    dy, ds = SLOTS[slot]
    return part_of((ka // 2 + dy) % 4, (ka % 2) ^ ds)


def exchange_pairs(slot):
    return [
        (block * 8 + ka, place(block, slot_part(ka, slot)))
        for block in range(32)
        for ka in range(8)
    ]


def x_pairs(odd):
    return [
        (place(block, part), place((block + (1 if block % 2 == odd else -1)) % 32, part))
        for block in range(32)
        for part in range(8)
    ]


def y_pairs(step):
    return [
        (place(block, 4 * half + part), place(block, 4 * half + (part + step) % 4))
        for block in range(32)
        for half in range(2)
        for part in range(4)
    ]


def middle_pairs(y):
    return [
        (place(block, part_of(y, half)), place(block, part_of(3, half)))
        for block in range(32)
        for half in range(2)
    ]


def send(value, pairs):
    return lax.ppermute(value, AXES, pairs)


def as_source():
    ka = lax.axis_index("ka")
    return ka >> 1, ka & 1


def as_host():
    gx, ka = lax.axis_index("gx"), lax.axis_index("ka")
    z = (ka & 1) * 4 + ((gx >> 1) & 3)
    turn = (z - 2) & 7
    return ka >> 1, (turn >> 2) ^ ((gx >> 3) & 1), (gx & 25) + (turn & 3) * 2


def part_index(y, half):
    return y + half * (7 - 2 * y)


def rows_to(slot):
    y, half = as_source()
    dy, ds = SLOTS[slot]
    return pl.ds(pl.multiple_of(part_index((y + dy) & 3, half ^ ds) * 8, 8), 8)


def kx_of(slot):
    y, half, block = as_host()
    dy, ds = SLOTS[slot]
    return pl.ds(pl.multiple_of((((y - dy) & 3) * 2 + (half ^ ds)) * 16, 16), 16)


def send_all(pieces, pairs, after):
    came = {}
    for slot in (0, 1, 2, 6, 7, 3, 4, 5):
        piece = pieces[slot]
        if slot in after:
            piece, came[after[slot]] = lax.optimization_barrier((piece, came[after[slot]]))
        came[slot] = send(piece, pairs(slot))
    return [came[slot] for slot in range(8)]


def halves(value):
    high = value.astype(BF16)
    return high, (value - high.astype(F32)).astype(BF16)


def circulant(row):
    return pltpu.roll(jnp.broadcast_to(row, (K, K)), 0, 1, stride=1, stride_axis=0)


def right_table(row):
    high, low = halves(circulant(row))
    return jnp.concatenate(
        [
            jnp.concatenate([high, low], 1),
            jnp.concatenate([high, jnp.zeros_like(low)], 1),
        ],
        0,
    )


def left_table(row):
    high, low = halves(circulant(row))
    return jnp.concatenate(
        [
            jnp.concatenate([high, high], 1),
            jnp.concatenate([low, jnp.zeros_like(low)], 1),
        ],
        0,
    )


def times_right(rows, table):
    both = jnp.dot(jnp.concatenate(halves(rows), 1), table, preferred_element_type=F32)
    return both[:, :K] + both[:, K:]


def times_left(table, first, second):
    high_0, low_0 = halves(first)
    high_1, low_1 = halves(second)
    stacked = jnp.concatenate(
        [jnp.concatenate([high_0, high_1], 1), jnp.concatenate([low_0, low_1], 1)], 0
    )
    both = jnp.dot(table, stacked, preferred_element_type=F32)
    both = both[:K] + both[K:]
    return both[:, :K], both[:, K:]


def slope(center, one, two):
    return 3.0 * center - 4.0 * one + two


def local_kernel(g_ref, ty_ref, vy_ref, out_ref, pad):
    vy = vy_ref[...].reshape(1, 1, K)
    toward = jnp.broadcast_to(vy > 0, (4, 16, K))
    rate = jnp.abs(vy) * 0.125

    def step(value, one_low, two_low, one_high, two_high, table):
        one = jnp.where(toward, one_low, one_high)
        two = jnp.where(toward, two_low, two_high)
        wigner = times_right(value.reshape(64, K), table).reshape(4, 16, K)
        return wigner - rate * slope(value, one, two)

    edge = jnp.zeros((4, 2, 16, K), F32)
    pad[0, :, 0:2] = edge
    pad[0, :, 66:68] = edge
    pad[1, :, 0:2] = edge
    pad[1, :, 66:68] = edge
    for y in range(64):
        pad[0, :, y + 2] = g_ref[:, y]

    def turn(source, into):
        @pl.loop(0, 8)
        def _(group):
            block = ty_ref[pl.ds(pl.multiple_of(group * 8, 8), 8), :]
            for inner in range(8):
                y = group * 8 + inner
                value = pad[source, :, y + 2]
                moved = step(
                    value,
                    pad[source, :, y + 1],
                    pad[source, :, y],
                    pad[source, :, y + 3],
                    pad[source, :, y + 4],
                    right_table(block[inner : inner + 1]),
                )
                into(y, value, moved)

    def first(y, value, moved):
        pad[1, :, y + 2] = value + moved

    def second(y, value, moved):
        out_ref[:, y] = 0.5 * (pad[0, :, y + 2] + value + moved)

    turn(0, first)
    turn(1, second)


def pack_kernel(g_ref, vel_ref, potential_ref, *pieces):
    y, half = as_source()
    for slot in range(8):
        at = rows_to(slot)
        for x in range(4):
            pieces[slot][8 * x : 8 * x + 8] = g_ref[x, at]
        pieces[slot][32] = vel_ref[...]
        dy, ds = SLOTS[slot]
        if dy == 0:
            at = pl.ds(32 - 2 * (half ^ ds), 2)
            for x in range(4):
                pieces[slot][33 + 2 * x : 35 + 2 * x] = g_ref[x, at]
    pieces[FIRST][41, 0:4] = potential_ref[...]
    pieces[FIRST][41, 4:16] = jnp.zeros((12, K), F32)


def across_kernel(first_ref, second_ref, out_ref):
    out_ref[0] = first_ref[33:41]
    out_ref[1] = second_ref[33:41]


def cut_kernel(*refs):
    pieces, (away_ref, near_ref, bottom_ref, top_ref) = refs[:8], refs[8:]
    core = lax.axis_index("gx") & 1
    for slot in range(8):
        away_ref[slot] = pieces[slot][pl.ds(core * 16, 16)]
        near_ref[slot] = pieces[slot][pl.ds(16 - core * 16, 16)]
        for x in range(4):
            bottom_ref[slot, 2 * x : 2 * x + 2] = pieces[slot][8 * x : 8 * x + 2]
            top_ref[slot, 2 * x : 2 * x + 2] = pieces[slot][8 * x + 6 : 8 * x + 8]


def inner_drift(center, x, layer, toward, rate):
    total = 3.0 * center
    for step, factor in ((1, -4.0), (2, 1.0)):
        low = layer(x - step) if x - step >= 0 else None
        high = layer(x + step) if x + step <= 3 else None
        if low is None:
            if high is not None:
                total += factor * jnp.where(toward, 0.0, high)
        elif high is None:
            total += factor * jnp.where(toward, low, 0.0)
        else:
            total += factor * jnp.where(toward, low, high)
    return -rate * total


def outer_drift(x, low, high, up, down):
    if x == 0:
        return up * (4.0 * low(0) - low(1))
    if x == 1:
        return -up * low(0)
    if x == 2:
        return -down * high(0)
    return down * (4.0 * high(0) - high(1))


def rates(vx_ref, at, factor):
    vx = vx_ref[at, :]
    block = as_host()[2]
    up = jnp.where(block == 0, 0.0, jnp.maximum(vx, 0.0) * factor)
    down = jnp.where(block == 31, 0.0, jnp.maximum(-vx, 0.0) * factor)
    return up[None], down[None]


def outer_layers(away_ref, near_ref, i):
    even = (lax.axis_index("gx") & 1) == 0

    def low(n):
        at = slice(8 - 8 * n, 16 - 8 * n)
        return jnp.where(even, away_ref[i, at], near_ref[i, at])

    def high(n):
        at = slice(8 * n, 8 * n + 8)
        return jnp.where(even, near_ref[i, at], away_ref[i, at])

    return low, high


def first_kernel(*refs):
    pieces, (sine_ref, ty_ref, vy_ref), (v_ref, vx_ref, tx_ref), (field, tables) = refs[:8], refs[8:11], refs[11:14], refs[14:]
    for slot in range(8):
        at = kx_of(slot)
        for x in range(4):
            field[x, :, at, :] = pieces[slot][8 * x : 8 * x + 8]
        vx_ref[at, :] = pieces[slot][32]
    tx_ref[...] = 0.25 * jnp.dot(
        pieces[FIRST][41, 0:8], sine_ref[...], precision=lax.Precision.HIGHEST, preferred_element_type=F32
    )
    for x in range(4):
        tables[x] = left_table(0.5 * tx_ref[x : x + 1, :])
    y_place, half, block = as_host()
    ty = ty_ref[pl.ds(pl.multiple_of(part_index(y_place, half) * 8, 8), 8), :]

    vx = vx_ref[...]
    toward = vx > 0
    rate = jnp.abs(vx) * 0.0625
    vy = jnp.broadcast_to(vy_ref[...], (K, K))
    toward_y = vy > 0
    rate_y = jnp.abs(vy) * 0.125
    zero = jnp.zeros((K, K), F32)
    for pair in range(4):
        right = [right_table(ty[pair * 2 + i : pair * 2 + i + 1, :]) for i in range(2)]
        for x in range(4):
            mine = [field[x, pair * 2 + i] for i in range(2)]
            wigner = times_left(tables[x], mine[0], mine[1])
            for i in range(2):
                y = pair * 2 + i
                total = mine[i] + wigner[i]
                total += inner_drift(mine[i], x, lambda at: field[at, y], toward, rate)
                total += times_right(mine[i], right[i])
                near = [field[x, at] if 0 <= at < 8 else zero for at in (y - 2, y - 1, y + 1, y + 2)]
                one = jnp.where(toward_y, near[1], near[2])
                two = jnp.where(toward_y, near[0], near[3])
                v_ref[x, y] = total - rate_y * slope(mine[i], one, two)


def first_edge_kernel(
    inner_ref, away_ref, near_ref, under_ref, over_ref, from_0_ref, from_1_ref, from_2_ref, own_0_ref, own_1_ref, vx_ref, vy_ref, v_ref, *outs
):
    y_place, half, block = as_host()
    middle = jnp.where(y_place == 3, 1.0, 0.0)
    under_middle, over_middle = y_place == 3 * half, y_place == 3 - 3 * half
    vy = vy_ref[...].reshape(1, 1, K)
    up_y = jnp.maximum(vy, 0.0) * 0.125
    down_y = jnp.maximum(-vy, 0.0) * 0.125

    def beside(ref, pair, rows):
        return ref[SLOTS.index(pair), rows]

    for slot in range(8):
        dy, ds = SLOTS[slot]
        at = kx_of(slot)
        up, down = rates(vx_ref, at, 0.0625)
        group = int(slot in GROUPS[1])
        i = GROUPS[group].index(slot)
        low, high = outer_layers(away_ref, near_ref, slot)
        even = (lax.axis_index("gx") & 1) == 0
        layers = []
        for x in range(4):
            rows = slice(2 * x, 2 * x + 2)
            if dy == 0:
                across = (own_0_ref, own_1_ref)[ds][33 + 2 * x : 35 + 2 * x]
            else:
                across = (from_2_ref, from_1_ref, from_0_ref)[dy - 1][ds, rows]
            before, after = ((dy + 3) % 4, ds), ((dy + 1) % 4, ds)
            under = jnp.where(half == 0, beside(under_ref, before, rows), beside(under_ref, after, rows))
            over = jnp.where(half == 0, beside(over_ref, after, rows), beside(over_ref, before, rows))
            under = jnp.where(under_middle, across * middle, under)
            over = jnp.where(over_middle, across * middle, over)
            value = inner_ref[x, :, at, :] + outer_drift(x, low, high, up, down)
            bottom = jnp.concatenate([up_y * (4.0 * under[1:2] - under[0:1]), -up_y * under[1:2]], 0)
            top = jnp.concatenate([-down_y * over[0:1], down_y * (4.0 * over[0:1] - over[1:2])], 0)
            value = jnp.concatenate([value[0:2] + bottom, value[2:6], value[6:8] + top], 0)
            v_ref[x, :, at, :] = value
            layers.append(value)
        near_out, away_out = outs[2 * group : 2 * group + 2]
        for x in range(2):
            at = slice(8 * x, 8 * x + 8)
            away_out[i, at] = jnp.where(even, layers[x], layers[x + 2])
            near_out[i, at] = jnp.where(even, layers[x + 2], layers[x])


def second_kernel(v_ref, tx_ref, vx_ref, out_ref, tables):
    for x in range(4):
        tables[x] = left_table(tx_ref[x : x + 1, :])

    @pl.loop(0, 4)
    def _(pair):
        vx = vx_ref[...]
        toward = vx > 0
        rate = jnp.abs(vx) * 0.125
        for x in range(4):
            mine = [v_ref[x, pair * 2 + i] for i in range(2)]
            wigner = times_left(tables[x], mine[0], mine[1])
            for i in range(2):
                y = pair * 2 + i
                out_ref[x, y] = wigner[i] + inner_drift(mine[i], x, lambda at: v_ref[at, y], toward, rate)


def second_edge_kernel(slots, inner_ref, one_ref, other_ref, vx_ref, *pieces):
    away_ref, near_ref = (other_ref, one_ref) if slots == GROUPS[0] else (one_ref, other_ref)
    for i, slot in enumerate(slots):
        at = kx_of(slot)
        up, down = rates(vx_ref, at, 0.125)
        low, high = outer_layers(away_ref, near_ref, i)
        for x in range(4):
            pieces[i][x] = inner_ref[x, :, at, :] + outer_drift(x, low, high, up, down)


def final_kernel(local_ref, *refs):
    pieces, (out_ref, total, sems) = refs[:8], refs[8:]
    copies = []
    for x in range(4):
        for slot in range(8):
            at = rows_to(slot)
            total[x, at] = local_ref[x, at] + pieces[slot][x]
        copies.append(pltpu.make_async_copy(total.at[x], out_ref.at[x], sems.at[x]))
        copies[-1].start()
    for copy in copies:
        copy.wait()


MIB = 1 << 20


def array(*shape):
    return jax.ShapeDtypeStruct(shape, F32)


def params():
    return pltpu.CompilerParams(vmem_limit_bytes=40 * MIB)


def cost(flops, mib):
    return pl.CostEstimate(flops=flops, bytes_accessed=mib * MIB, transcendentals=0)


def call(kernel, outs, scratch=(), flops=0, mib=4, ins=None, out_specs=None):
    def run(*operands):
        return pl.pallas_call(
            kernel,
            out_shape=outs,
            in_specs=ins or [VMEM] * len(operands),
            out_specs=out_specs or ([VMEM] * len(outs) if isinstance(outs, list) else VMEM),
            scratch_shapes=list(scratch),
            compiler_params=params(),
            cost_estimate=cost(flops, mib),
            name=kernel.func.__name__ if isinstance(kernel, functools.partial) else kernel.__name__,
        )(*operands)

    return run


def sine_table(sign):
    index = np.arange(K)
    angle = (sign * index[:, None] * index[None, :] % K) * (2.0 * math.pi / K)
    return (np.sin(angle) / K).astype(np.float32)


def back(pairs):
    return [(there, here) for here, there in pairs]


def per_device(density, potential_x, potential_y, speeds_x, speeds_y, upwind_x, upwind_y):
    vel_x = (2 * upwind_x - 1).astype(F32) * speeds_x
    vel_x = jnp.broadcast_to(vel_x[:, None], (16, K))
    vy = ((2 * upwind_y - 1).astype(F32) * speeds_y).reshape(1, K)

    sizes = [33 + 8 * (dy == 0) + (slot == FIRST) for slot, (dy, ds) in enumerate(SLOTS)]
    pieces = call(pack_kernel, [array(size, 16, K) for size in sizes])(density, vel_x, potential_x)
    pieces = send_all(pieces, exchange_pairs, {3: 7, 4: 6, 5: 1})

    highest = lax.Precision.HIGHEST
    ty = 0.25 * jnp.dot(potential_y, jnp.asarray(sine_table(1)), precision=highest)
    local = call(
        local_kernel, array(4, 64, 16, K), [pltpu.VMEM((2, 4, 68, 16, K), F32)], 4 * 10**9
    )(density, ty, vy)

    across = call(across_kernel, array(2, 8, 16, K), mib=0)(pieces[FIRST], pieces[SECOND])
    across = [send(across, middle_pairs(y)) for y in range(3)]
    *pieces, across[0], across[1], across[2] = lax.optimization_barrier((*pieces, *across))
    away, near, bottom, top = call(cut_kernel, [array(8, 16, 16, K)] * 2 + [array(8, 8, 16, K)] * 2)(*pieces)
    near, away = send(near, x_pairs(0)), send(away, x_pairs(1))
    under, over = send(top, y_pairs(1)), send(bottom, y_pairs(-1))
    left_tables = pltpu.VMEM((4, 2 * K, 2 * K), BF16)
    inner, vx, tx = call(
        first_kernel,
        [array(4, 8, K, K), array(K, K), array(8, K)],
        [pltpu.VMEM((4, 8, K, K), F32), left_tables],
        3 * 10**9,
    )(*pieces, jnp.asarray(sine_table(-1)), ty, vy)
    v, *sides = call(first_edge_kernel, [array(4, 8, K, K)] + [array(4, 16, 16, K)] * 4)(
        inner, away, near, under, over, *across, pieces[FIRST], pieces[SECOND], vx, vy
    )
    away = [send(sides[2 * group + 1], x_pairs(1)) for group in range(2)]
    near = [send(sides[2 * group], x_pairs(0)) for group in range(2)]
    inner = call(second_kernel, array(4, 8, K, K), [left_tables], 2 * 10**9)(v, tx, vx)
    pieces = [None] * 8
    for group, slots in enumerate(GROUPS):
        cut = call(functools.partial(second_edge_kernel, slots), [array(4, 8, 16, K)] * 4, mib=2)(
            inner, *((near[0], away[0]) if group == 0 else (away[1], near[1])), vx
        )
        for slot, piece in zip(slots, cut):
            pieces[slot] = piece
    pieces = send_all(pieces, lambda slot: back(exchange_pairs(slot)), {3: 6, 4: 7, 5: 0})

    return call(
        final_kernel,
        array(4, 64, 16, K),
        [pltpu.VMEM((4, 64, 16, K), F32), pltpu.SemaphoreType.DMA((4,))],
        out_specs=HBM,
    )(local, *pieces)


def solution(mesh):
    in_specs = (P("gx", None, "ka", None), P("gx", None), P(), P("ka"), P(), P("ka"), P())
    out_specs = P("gx", None, "ka", None)
    return jax.shard_map(
        per_device, mesh=mesh, in_specs=in_specs, out_specs=out_specs, check_vma=False
    )
```
